512 devices in a mesh: wide: 128 (over z, x, core), narrow: 4 (over y).
Axes of the slice: x: 4, y: 4, z: 16, core: 2. Of those that a mesh axis runs over, the one named last changes fastest.
Arguments:
- state: float32 [2, 33554432], P(None, ('wide', 'narrow')), may hold values from -6 to 6
- gates: float32 [8, 2, 128, 128], replicated, may hold values from -1 to 1, as said below
- gate_qubits: int32 [8, 7], replicated, may hold values from 7 to 15, as said below
- swap_order: int32 [9], replicated, may hold values from 7 to 15, as said below
Outputs:
- checkpoint: float32 [2, 33554432], P(None, ('wide', 'narrow'))
The draws below stay inside these ranges and needn't reach their ends.
Inputs may be any that keep to these rules, and one draw needn't show every extreme that they name: `gate_qubits`: each row names 7 different qubits. `swap_order`: each number of the range appears once. Each gates[g, 0] + i gates[g, 1] is a unitary matrix.
All inputs are finite; a program needn't handle non-finite values.
Results may differ from the reference program's by a relative error of at most 0.0003.
Values sent between devices are 32-bit elements; how exact they have to be, the bound alone decides.
No kernel may reach another device: no remote copies, remote signals or barrier semaphores. Data moves between devices by JAX's collectives and lax.ppermute only.
A program may use at most 64 MiB of HBM per device.

```python
import math
import jax
import jax.numpy as jnp
from jax import lax

AMP_DEV = 65536
GATE_QUBITS = 7
LANE_QUBITS = 7
GATES = 8
GATE_DIM = 128
LOCAL_QUBITS = 16
NAMPS = 33554432
N_WIDE = 128
N_NARROW = 4


def orthonormal(matrix_pair):
    source_real = matrix_pair[0]
    source_imag = matrix_pair[1]
    extent = source_real.shape[0]

    def column_step(column, frames):
        frame_real, frame_imag = frames
        vector_real = lax.dynamic_index_in_dim(source_real, column, 1, keepdims=False)
        vector_imag = lax.dynamic_index_in_dim(source_imag, column, 1, keepdims=False)
        for repeat in range(2):
            weight_real = jnp.dot(frame_real.T, vector_real, precision=lax.Precision.HIGHEST) + jnp.dot(frame_imag.T, vector_imag, precision=lax.Precision.HIGHEST)
            weight_imag = jnp.dot(frame_real.T, vector_imag, precision=lax.Precision.HIGHEST) - jnp.dot(frame_imag.T, vector_real, precision=lax.Precision.HIGHEST)
            vector_real = vector_real - (jnp.dot(frame_real, weight_real, precision=lax.Precision.HIGHEST) - jnp.dot(frame_imag, weight_imag, precision=lax.Precision.HIGHEST))
            vector_imag = vector_imag - (jnp.dot(frame_real, weight_imag, precision=lax.Precision.HIGHEST) + jnp.dot(frame_imag, weight_real, precision=lax.Precision.HIGHEST))
        length = jnp.sqrt(jnp.sum(vector_real * vector_real + vector_imag * vector_imag))
        frame_real = lax.dynamic_update_index_in_dim(frame_real, vector_real / length, column, 1)
        frame_imag = lax.dynamic_update_index_in_dim(frame_imag, vector_imag / length, column, 1)
        return (frame_real, frame_imag)
    zeros_block = jnp.zeros((extent, extent), jnp.float32)
    frames = lax.fori_loop(0, extent, column_step, (zeros_block, zeros_block))
    return jnp.stack([frames[0], frames[1]])


def draw_gates(key, part):
    samples = jax.random.normal(jax.random.fold_in(key, 5), (GATES, 2, GATE_DIM, GATE_DIM), jnp.float32)
    return jax.vmap(orthonormal)(samples).astype(jnp.float32)


def draw_gate_qubits(key, part):
    subkeys = jax.random.split(jax.random.fold_in(key, 11), GATES)
    upper_count = LOCAL_QUBITS - LANE_QUBITS
    chosen = jax.vmap(lambda single: jax.random.permutation(single, upper_count)[:GATE_QUBITS])(subkeys)
    return (chosen + LANE_QUBITS).astype(jnp.int32)


def draw_swap_order(key, part):
    upper_count = LOCAL_QUBITS - LANE_QUBITS
    ordering = jax.random.permutation(jax.random.fold_in(key, 17), upper_count)
    return (ordering + LANE_QUBITS).astype(jnp.int32)


def level_of(key, dims, cuts, low, high):
    gain = 1.0
    for dim, blocks in cuts:
        steps = jax.random.uniform(jax.random.fold_in(jax.random.fold_in(key, 6), dim), (blocks,), jnp.float32, low / len(cuts), high / len(cuts))
        gain = gain * jnp.repeat(jnp.exp(steps), dims[dim] // blocks).reshape((-1,) + (1,) * (len(dims) - 1 - dim))
    return gain


def noise(key, shape, spread, most, shards=(), kind=jnp.bfloat16):
    array = jax.random.normal(key, shape, jnp.float32) * spread
    if len(shards) > 0:
        array = level_of(key, shape, shards, -0.22, 0.18) * array
    return jnp.clip(array, min=-most, max=most).astype(kind)


def setup_inputs(seed: int = 0) -> dict:
    keys = jax.random.split(jax.random.key(seed), 5)
    return {
        "state": noise(keys[0], (2, NAMPS), 1.0, 6.0, ((1, 512),), jnp.float32),
        "gates": draw_gates(jax.random.fold_in(keys[4], 71), 0),
        "gate_qubits": draw_gate_qubits(jax.random.fold_in(keys[4], 71), 0),
        "swap_order": draw_swap_order(jax.random.fold_in(keys[4], 71), 0),
    }


companding = 16.0
companding_norm = math.log(16.0 + math.sqrt(257.0))

def inverse_sinh(values):
    magnitude = jnp.abs(values)
    squared = magnitude * magnitude
    return jnp.sign(values) * jnp.log1p(magnitude + squared / (1.0 + jnp.sqrt(squared + 1.0)))

def shuffle_index(source, target, qubit_count):
    position = jnp.argsort(source).astype(jnp.int32)
    shifts = position[target].astype(jnp.int32)
    low_count = qubit_count // 2
    high_count = qubit_count - low_count
    low_values = jnp.arange(2 ** low_count, dtype=jnp.int32)
    high_values = jnp.arange(2 ** high_count, dtype=jnp.int32)
    low_bits = jnp.right_shift(low_values[:, None], jnp.arange(low_count, dtype=jnp.int32)[None, :]) & 1
    high_bits = jnp.right_shift(high_values[:, None], jnp.arange(high_count, dtype=jnp.int32)[None, :]) & 1
    low_part = lax.optimization_barrier(jnp.sum(jnp.left_shift(low_bits, shifts[None, :low_count]), axis=1)).astype(jnp.int32)
    high_part = lax.optimization_barrier(jnp.sum(jnp.left_shift(high_bits, shifts[None, low_count:]), axis=1)).astype(jnp.int32)
    return (high_part[:, None] + low_part[None, :]).reshape(-1).astype(jnp.int32)

def gate_order(chosen, qubit_count):
    ranking = jnp.arange(qubit_count, dtype=jnp.int32) + qubit_count
    ranking = ranking.at[chosen].set(jnp.arange(chosen.shape[0], dtype=jnp.int32))
    return jnp.argsort(ranking).astype(jnp.int32)

def top_order(chosen, qubit_count):
    ranking = jnp.arange(qubit_count, dtype=jnp.int32)
    ranking = ranking.at[chosen].set(qubit_count + jnp.arange(chosen.shape[0], dtype=jnp.int32))
    return jnp.argsort(ranking).astype(jnp.int32)

def gate_blocks(matrix):
    real_part = matrix[0]
    imag_part = matrix[1]
    return jnp.stack([jnp.stack([real_part, imag_part]), jnp.stack([-imag_part, real_part])])

def apply_local(values, matrix):
    shaped = values.reshape(2, -1, matrix.shape[-1])
    mixed = jnp.einsum('crb,cdab->dra', shaped, gate_blocks(matrix), precision=lax.Precision.HIGHEST)
    return mixed.reshape(values.shape)

def reference_gate(amplitudes, matrix, chosen):
    natural = jnp.arange(LOCAL_QUBITS, dtype=jnp.int32)
    layout = gate_order(chosen, LOCAL_QUBITS)
    arranged = jnp.take(amplitudes, shuffle_index(natural, layout, LOCAL_QUBITS), axis=2)
    mixed = apply_local(arranged, matrix)
    return jnp.take(mixed, shuffle_index(layout, natural, LOCAL_QUBITS), axis=2)

def reference_swap(amplitudes, chosen, group_count, first_axis):
    natural = jnp.arange(LOCAL_QUBITS, dtype=jnp.int32)
    layout = top_order(chosen, LOCAL_QUBITS)
    arranged = jnp.take(amplitudes, shuffle_index(natural, layout, LOCAL_QUBITS), axis=2)
    grid = arranged.reshape(2, N_WIDE, N_NARROW, group_count, AMP_DEV // group_count)
    grid = jnp.swapaxes(grid, first_axis, 3)
    arranged = grid.reshape(2, N_WIDE * N_NARROW, AMP_DEV)
    return jnp.take(arranged, shuffle_index(layout, natural, LOCAL_QUBITS), axis=2)

def reference(state, gates, gate_qubits, swap_order):
    wide_bits = N_WIDE.bit_length() - 1
    narrow_bits = N_NARROW.bit_length() - 1
    upper_count = LOCAL_QUBITS - LANE_QUBITS
    amplitudes = state.reshape(2, N_WIDE * N_NARROW, AMP_DEV)
    for number in range(3):
        amplitudes = reference_gate(amplitudes, gates[number], gate_qubits[number])
    amplitudes = reference_swap(amplitudes, swap_order[upper_count - wide_bits:], N_WIDE, 1)
    for number in range(3, 6):
        amplitudes = reference_gate(amplitudes, gates[number], gate_qubits[number])
    amplitudes = reference_swap(amplitudes, swap_order[:narrow_bits], N_NARROW, 2)
    for number in range(6, 8):
        amplitudes = reference_gate(amplitudes, gates[number], gate_qubits[number])
    final = amplitudes.reshape(2, -1)
    highest = jnp.max(final)
    lowest = jnp.min(final)
    middle = (highest + lowest) * 0.5
    halfwidth = (highest - lowest) * 0.5 + 1e-06
    return inverse_sinh(companding * (final - middle) / halfwidth) / companding_norm
```

```python
import functools
import math

import jax
import jax.numpy as jnp
from jax import lax
from jax.experimental import pallas as pl
from jax.experimental.pallas import tpu as pltpu
from jax.sharding import Mesh
from jax.sharding import PartitionSpec as P

LANE_QUBITS = 7
UPPER = 9
ROWS = 2**UPPER
DIM = 128
Z, XCY = "z", ("x", "core", "narrow")
ALL = ("z", "x", "core", "narrow")

F32, BF16, I32 = jnp.float32, jnp.bfloat16, jnp.int32
companding = 16.0
companding_norm = math.log(16.0 + math.sqrt(257.0))
VMEM_LIMIT = 40 * 2**20


def dot(a, b):
    return jnp.dot(a, b, preferred_element_type=F32)


def pieces(x):
    high = x.astype(BF16)
    return high, (x - high.astype(F32)).astype(BF16)


def gate_layout(gate_qubits, gate):
    chosen = [gate_qubits[gate, k] - LANE_QUBITS for k in range(7)]
    used = sum(lax.shift_left(I32(1), c) for c in chosen)
    low, high = I32(0), I32(0)
    for row_bit in range(UPPER):
        free = (lax.shift_right_logical(used, I32(row_bit)) & 1) == 0
        low = jnp.where(free & (high == 0) & (low == 0), row_bit + 100, low)
        high = jnp.where(free, row_bit, high)
    return chosen + [low - 100, high]


def swap_layout(swap_order):
    order = [swap_order[k] - LANE_QUBITS for k in range(UPPER)]
    return order[2:] + order[:2]


def permutation(source, target, place):
    if target is not None:
        for b in range(UPPER):
            place[target[b]] = I32(b)
    index = lax.broadcasted_iota(I32, (1, ROWS), 1)
    moved = jnp.zeros((1, ROWS), I32)
    for b in range(UPPER):
        row_bit = b if source is None else source[b]
        to = row_bit if target is None else place[row_bit]
        moved = moved + (lax.shift_right_logical(index, b) & 1) * lax.shift_left(I32(1), I32(to))
    rows = lax.broadcasted_iota(I32, (ROWS, ROWS), 0)
    return jnp.where(rows == moved, 1.0, 0.0).astype(BF16)


def gate_matrix(gates_ref, gate):
    real, imag = gates_ref[gate, 0], gates_ref[gate, 1]
    top = jnp.concatenate([real, -imag], axis=1)
    bottom = jnp.concatenate([imag, real], axis=1)
    high, low = pieces(jnp.concatenate([top, bottom], axis=0))
    return jnp.concatenate([high, low], axis=0)


def apply_gate(matrix, high, low):
    width = high.shape[1] // 2
    size = 2 * DIM
    done = []
    for other in range(ROWS // DIM):
        rows = slice(other * DIM, (other + 1) * DIM)
        stacked = jnp.concatenate([high[rows, :width], high[rows, width:]], axis=0)
        both = dot(matrix, stacked)
        mixed = both[:size] + both[size:]
        if low is not None:
            rest = jnp.concatenate([low[rows, :width], low[rows, width:]], axis=0)
            mixed = mixed + dot(matrix[:size], rest)
        done.append(jnp.concatenate([mixed[:DIM], mixed[DIM:]], axis=1))
    return jnp.concatenate(done, axis=0)


def permute(matrix, high, low):
    return dot(matrix, high).astype(BF16), dot(matrix, low).astype(BF16)


def quarters(slabs):
    lane = lax.broadcasted_iota(I32, slabs[0].shape, 1)
    first = lane < 64
    half = [None] * 4
    for i in range(2):
        half[i] = jnp.where(first, slabs[i], pltpu.roll(slabs[i + 2], 64, 1))
        half[i + 2] = jnp.where(first, pltpu.roll(slabs[i], 64, 1), slabs[i + 2])
    even = (lane & 32) == 0
    out = [None] * 4
    for i in (0, 2):
        out[i] = jnp.where(even, half[i], pltpu.roll(half[i + 1], 32, 1))
        out[i + 1] = jnp.where(even, pltpu.roll(half[i], 96, 1), half[i + 1])
    return out


def slabs_of(x):
    return [x[DIM * i : DIM * (i + 1)] for i in range(4)]


def first_kernel(gate_qubits, swap_order, state_ref, gates_ref, out_ref, place):
    planes = [state_ref[pl.ds(p, ROWS, stride=2), :] for p in range(2)]
    high, low = pieces(jnp.concatenate(planes, axis=1))
    layout = None
    for gate in range(3):
        target = gate_layout(gate_qubits, gate)
        high, low = permute(permutation(layout, target, place), high, low)
        layout = target
        high, low = pieces(apply_gate(gate_matrix(gates_ref, gate), high, low))
    matrix = permutation(layout, swap_layout(swap_order), place)
    mixed = dot(matrix, high) + dot(matrix, low)
    for p in range(2):
        for y, slab in enumerate(quarters(slabs_of(mixed[:, DIM * p : DIM * (p + 1)]))):
            out_ref[pl.ds(2 * y + p, DIM, stride=8), :] = slab


def compose_kernel(gate_qubits, swap_order, gates_ref, second_ref, third_ref, place):
    swapped = swap_layout(swap_order)
    for out_ref, numbers, last in ((second_ref, (3, 4, 5), swapped), (third_ref, (6, 7), None)):
        layout = swapped
        for gate in numbers:
            target = gate_layout(gate_qubits, gate)
            matrix = permutation(layout, target, place)
            if gate == numbers[0]:
                high = jnp.concatenate([matrix, jnp.zeros_like(matrix)], axis=1)
                low = None
            else:
                high, low = permute(matrix, high, low)
            layout = target
            high, low = pieces(apply_gate(gate_matrix(gates_ref, gate), high, low))
        high, low = permute(permutation(layout, last, place), high, low)
        for number, part in enumerate((high[:, :ROWS], high[:, ROWS:], low[:, :ROWS], low[:, ROWS:])):
            out_ref[ROWS * number : ROWS * (number + 1), :] = part


def apply_matrix(matrix_ref, real, imag):
    high, low = pieces(jnp.concatenate([real, imag], axis=1))
    both = dot(matrix_ref[...], high)
    total = both[: 2 * ROWS] + both[2 * ROWS :] + dot(matrix_ref[: 2 * ROWS, :], low)
    return (
        total[:ROWS, :DIM] - total[ROWS:, DIM:],
        total[ROWS:, :DIM] + total[:ROWS, DIM:],
    )


def middle_kernel(arrived_ref, second_ref, third_ref, out_ref, extremes_ref):
    planes = [
        jnp.concatenate(
            quarters([arrived_ref[pl.ds(2 * n + p, DIM, stride=8), :] for n in range(4)]), axis=0
        )
        for p in range(2)
    ]
    planes = apply_matrix(second_ref, *planes)
    planes = [jnp.concatenate(quarters(slabs_of(x)), axis=0) for x in planes]
    planes = apply_matrix(third_ref, *planes)
    highest = jnp.max(jnp.maximum(planes[0], planes[1]))
    lowest = jnp.min(jnp.minimum(planes[0], planes[1]))
    lane = lax.broadcasted_iota(I32, extremes_ref.shape, 1)
    extremes_ref[...] = jnp.where(lane < 64, highest, -lowest)
    for p in range(2):
        for t, slab in enumerate(quarters(slabs_of(planes[p]))):
            out_ref[t, p] = slab


def last_kernel(extremes_ref, arrived_ref, out_ref):
    lane = lax.broadcasted_iota(I32, extremes_ref.shape, 1)
    found = extremes_ref[...]
    least = jnp.min(found)
    highest = jnp.max(jnp.where(lane < 64, found, least))
    lowest = -jnp.max(jnp.where(lane < 64, least, found))
    middle = (highest + lowest) * 0.5
    halfwidth = (highest - lowest) * 0.5 + 1e-06
    for p in range(2):
        for q, slab in enumerate(quarters([arrived_ref[y, p] for y in range(4)])):
            value = companding * (slab - middle) / halfwidth
            size = jnp.abs(value)
            curve = jnp.log(size + jnp.sqrt(size * size + 1.0)) / companding_norm
            out_ref[pl.ds(2 * DIM * q + p, DIM, stride=2), :] = jnp.where(value < 0, -curve, curve)


def call(kernel, inputs, outs, places, scratch=(), flops=0, gates=False):
    return pl.pallas_call(
        kernel,
        out_shape=outs,
        in_specs=[pl.BlockSpec(memory_space=m) for m in places],
        scratch_shapes=scratch,
        compiler_params=pltpu.CompilerParams(vmem_limit_bytes=VMEM_LIMIT),
        cost_estimate=pl.CostEstimate(flops=flops, bytes_accessed=2**20, transcendentals=0),
    )(*inputs)


def exchange(array, axes):
    return lax.all_to_all(array, axes, split_axis=0, concat_axis=0, tiled=True)


def local(state, gates, gate_qubits, swap_order):
    scalars, vectors = [pltpu.SMEM] * 2, pltpu.VMEM
    place = [pltpu.SMEM((16,), I32)]
    rows = state.reshape(2, ROWS, DIM).transpose(1, 0, 2).reshape(2 * ROWS, DIM)
    sent = call(
        first_kernel,
        (gate_qubits, swap_order, rows, gates),
        jax.ShapeDtypeStruct((2 * ROWS, DIM), F32),
        [*scalars, vectors, vectors],
        place,
        3 * 10**9,
    )
    count = lax.axis_size(ALL)
    arrived = exchange(sent.reshape(count, -1, DIM), ALL).reshape(2 * ROWS, DIM)
    matrix = jax.ShapeDtypeStruct((4 * ROWS, ROWS), BF16)
    second, third = call(
        compose_kernel,
        (gate_qubits, swap_order, gates),
        [matrix, matrix],
        [*scalars, vectors],
        place,
        10**10,
    )
    narrow, tall = lax.axis_size("narrow"), lax.axis_size(Z)
    blocks, extremes = call(
        middle_kernel,
        (arrived, second, third),
        [
            jax.ShapeDtypeStruct((narrow, 2, DIM, DIM), F32),
            jax.ShapeDtypeStruct((tall, DIM), F32),
        ],
        [vectors] * 3,
        (),
        2 * 10**9,
    )
    extremes = exchange(extremes.reshape(tall, 1, DIM), Z)
    others = lax.axis_size(XCY)
    extremes = jnp.broadcast_to(jnp.max(extremes, axis=0, keepdims=True), (others, 1, DIM))
    extremes = exchange(extremes, XCY).reshape(others, DIM)
    returned = exchange(blocks, "narrow")
    out = call(
        last_kernel,
        (extremes, returned),
        jax.ShapeDtypeStruct((2 * ROWS, DIM), F32),
        [vectors] * 2,
        (),
        10**7,
    )
    return out.reshape(ROWS, 2, DIM).transpose(1, 0, 2).reshape(2, -1)


def solution(mesh):
    split = Mesh(mesh.devices.reshape(16, 4, 2, mesh.shape["narrow"]), ALL)
    return jax.shard_map(
        local,
        mesh=split,
        in_specs=(P(None, ALL), P(), P(), P()),
        out_specs=P(None, ALL),
        check_vma=False,
    )
```

```python
import functools
import math

import jax
import jax.numpy as jnp
from jax import lax
from jax.experimental import pallas as pl
from jax.experimental.pallas import tpu as pltpu
from jax.sharding import Mesh
from jax.sharding import PartitionSpec as P

LANE_QUBITS = 7
UPPER = 9
ROWS = 2**UPPER
DIM = 128
TAIL = 8
OTHERS = ("x", "core", "z")
ALL = ("z", "x", "core", "narrow")
SENT = ("x", "core", "narrow", "z")

F32, BF16, I32 = jnp.float32, jnp.bfloat16, jnp.int32
companding = 16.0
companding_norm = math.log(16.0 + math.sqrt(257.0))
VMEM_LIMIT = 40 * 2**20
MIDDLE_LIMIT = 58 * 2**20
LARGE_LIMIT = 60 * 2**20


def dot(a, b):
    return jnp.dot(a, b, preferred_element_type=F32)


def pieces(x):
    high = x.astype(BF16)
    return high, (x - high.astype(F32)).astype(BF16)


def gate_layout(gate_qubits, gate):
    chosen = [gate_qubits[gate, k] - LANE_QUBITS for k in range(7)]
    used = sum(lax.shift_left(I32(1), c) for c in chosen)
    low, high = I32(0), I32(0)
    for row_bit in range(UPPER):
        free = (lax.shift_right_logical(used, I32(row_bit)) & 1) == 0
        low = jnp.where(free & (high == 0) & (low == 0), row_bit + 100, low)
        high = jnp.where(free, row_bit, high)
    return chosen + [low - 100, high]


def swap_layout(swap_order):
    order = [swap_order[k] - LANE_QUBITS for k in range(UPPER)]
    return order[5:] + order[2:5] + order[:2]


def permutation(source, target, place):
    if target is not None:
        for b in range(UPPER):
            place[target[b]] = I32(b)
    index = lax.broadcasted_iota(I32, (1, ROWS), 1)
    moved = jnp.zeros((1, ROWS), I32)
    for b in range(UPPER):
        row_bit = b if source is None else source[b]
        to = row_bit if target is None else place[row_bit]
        moved = moved + (lax.shift_right_logical(index, b) & 1) * lax.shift_left(I32(1), I32(to))
    rows = lax.broadcasted_iota(I32, (ROWS, ROWS), 0)
    return jnp.where(rows == moved, 1.0, 0.0).astype(BF16)


def gate_matrix(gates_ref, gate):
    real, imag = gates_ref[gate, 0], gates_ref[gate, 1]
    top = jnp.concatenate([real, -imag], axis=1)
    bottom = jnp.concatenate([imag, real], axis=1)
    high, low = pieces(jnp.concatenate([top, bottom], axis=0))
    return jnp.concatenate([high, low], axis=0)


def apply_gate(matrix, high, low):
    width = high.shape[1] // 2
    size = 2 * DIM

    def stack(part):
        blocks = [part[DIM * i : DIM * (i + 1)] for i in range(4)]
        real = jnp.concatenate([block[:, :width] for block in blocks], axis=1)
        imag = jnp.concatenate([block[:, width:] for block in blocks], axis=1)
        return jnp.concatenate([real, imag], axis=0)

    both = dot(matrix, stack(high))
    mixed = both[:size] + both[size:]
    if low is not None:
        mixed = mixed + dot(matrix[:size], stack(low))
    columns = [mixed[:, width * i : width * (i + 1)] for i in range(4)]
    return jnp.concatenate(
        [jnp.concatenate([c[:DIM], c[DIM:]], axis=1) for c in columns], axis=0
    )


def permute(matrix, high, low):
    return dot(matrix, high).astype(BF16), dot(matrix, low).astype(BF16)


def quarters(slabs):
    lane = lax.broadcasted_iota(I32, slabs[0].shape, 1)
    first = lane < 64
    half = [None] * 4
    for i in range(2):
        half[i] = jnp.where(first, slabs[i], pltpu.roll(slabs[i + 2], 64, 1))
        half[i + 2] = jnp.where(first, pltpu.roll(slabs[i], 64, 1), slabs[i + 2])
    even = (lane & 32) == 0
    out = [None] * 4
    for i in (0, 2):
        out[i] = jnp.where(even, half[i], pltpu.roll(half[i + 1], 32, 1))
        out[i + 1] = jnp.where(even, pltpu.roll(half[i], 96, 1), half[i + 1])
    return out


def slabs_of(x):
    return [x[DIM * i : DIM * (i + 1)] for i in range(4)]


def first_kernel(
    gate_qubits, swap_order, state_hbm, gates_hbm, out_ref, state_ref, gates_ref, place, done
):
    state_copy = pltpu.make_async_copy(state_hbm, state_ref, done.at[0])
    gates_copy = pltpu.make_async_copy(gates_hbm.at[pl.ds(0, 3)], gates_ref, done.at[1])
    state_copy.start()
    gates_copy.start()
    state_copy.wait()
    gates_copy.wait()
    planes = [state_ref[pl.ds(p, ROWS, stride=2), :] for p in range(2)]
    high, low = pieces(jnp.concatenate(planes, axis=1))
    layout = None
    for gate in range(3):
        target = gate_layout(gate_qubits, gate)
        high, low = permute(permutation(layout, target, place), high, low)
        layout = target
        high, low = pieces(apply_gate(gate_matrix(gates_ref, gate), high, low))
    matrix = permutation(layout, swap_layout(swap_order), place)
    mixed = dot(matrix, high) + dot(matrix, low)
    for p in range(2):
        for y, slab in enumerate(quarters(slabs_of(mixed[:, DIM * p : DIM * (p + 1)]))):
            for block in range(8):
                rows = slab[16 * block : 16 * (block + 1)]
                out_ref[pl.ds(128 * block + 32 * y + p, 16, stride=2), :] = rows


def compose_kernel(gate_qubits, swap_order, gates_ref, out_ref, place):
    swapped = swap_layout(swap_order)
    for start, numbers, last in ((0, (3, 4, 5), swapped), (4 * ROWS, (6, 7), None)):
        layout = swapped
        for gate in numbers:
            target = gate_layout(gate_qubits, gate)
            matrix = permutation(layout, target, place)
            if gate == numbers[0]:
                high = jnp.concatenate([matrix, jnp.zeros_like(matrix)], axis=1)
                low = None
            else:
                high, low = permute(matrix, high, low)
            layout = target
            high, low = pieces(apply_gate(gate_matrix(gates_ref, gate), high, low))
        high, low = permute(permutation(layout, last, place), high, low)
        for number, part in enumerate((high[:, :ROWS], high[:, ROWS:], low[:, :ROWS], low[:, ROWS:])):
            out_ref[start + ROWS * number : start + ROWS * (number + 1), :] = part


def apply_matrix(matrix_ref, real, imag):
    high, low = pieces(jnp.concatenate([real, imag], axis=1))
    both = dot(matrix_ref[...], high)
    total = both[: 2 * ROWS] + both[2 * ROWS :] + dot(matrix_ref[: 2 * ROWS, :], low)
    return (
        total[:ROWS, :DIM] - total[ROWS:, DIM:],
        total[ROWS:, :DIM] + total[:ROWS, DIM:],
    )


def middle_kernel(
    arrived_ref, matrices_hbm, out_ref, second_ref, third_ref, done
):
    second_copy = pltpu.make_async_copy(
        matrices_hbm.at[pl.ds(0, 4 * ROWS)], second_ref, done.at[0])
    third_copy = pltpu.make_async_copy(
        matrices_hbm.at[pl.ds(4 * ROWS, 4 * ROWS)], third_ref, done.at[1])
    second_copy.start()
    third_copy.start()
    planes = []
    for p in range(2):
        slabs = []
        for n in range(4):
            starts = [128 * block + 32 * n + p for block in range(8)]
            rows = [arrived_ref[pl.ds(start, 16, stride=2), :] for start in starts]
            slabs.append(jnp.concatenate(rows, axis=0))
        planes.append(jnp.concatenate(quarters(slabs), axis=0))
    second_copy.wait()
    planes = apply_matrix(second_ref, *planes)
    planes = [jnp.concatenate(quarters(slabs_of(x)), axis=0) for x in planes]
    third_copy.wait()
    planes = apply_matrix(third_ref, *planes)
    highest = jnp.max(jnp.maximum(planes[0], planes[1]))
    lowest = jnp.min(jnp.minimum(planes[0], planes[1]))
    lane = lax.broadcasted_iota(I32, (TAIL, DIM), 1)
    extremes = jnp.where(lane < 64, highest, -lowest)
    for p in range(2):
        for t, slab in enumerate(quarters(slabs_of(planes[p]))):
            out_ref[t, DIM * p : DIM * (p + 1), :] = slab
    for t in range(4):
        out_ref[t, 2 * DIM : 2 * DIM + TAIL, :] = extremes


def reduce_kernel(arrived_ref, out_ref):
    found = jnp.max(
        jnp.max(arrived_ref[:, 2 * DIM : 2 * DIM + TAIL, :], axis=0), axis=0, keepdims=True
    )
    out_ref[...] = jnp.broadcast_to(found, out_ref.shape)


def last_kernel(extremes_ref, arrived_ref, out_ref):
    lane = lax.broadcasted_iota(I32, extremes_ref.shape, 1)
    found = extremes_ref[...]
    least = jnp.min(found)
    highest = jnp.max(jnp.where(lane < 64, found, least))
    lowest = -jnp.max(jnp.where(lane < 64, least, found))
    middle = (highest + lowest) * 0.5
    halfwidth = (highest - lowest) * 0.5 + 1e-06
    for p in range(2):
        for q, slab in enumerate(quarters([arrived_ref[y, DIM * p : DIM * (p + 1), :] for y in range(4)])):
            value = companding * (slab - middle) / halfwidth
            size = jnp.abs(value)
            curve = jnp.log(size + jnp.sqrt(size * size + 1.0)) / companding_norm
            out_ref[pl.ds(2 * DIM * q + p, DIM, stride=2), :] = jnp.where(value < 0, -curve, curve)


def call(kernel, inputs, outs, places, scratch=(), flops=0, limit=VMEM_LIMIT):
    return pl.pallas_call(
        kernel,
        out_shape=outs,
        in_specs=[pl.BlockSpec(memory_space=m) for m in places],
        scratch_shapes=scratch,
        compiler_params=pltpu.CompilerParams(vmem_limit_bytes=limit),
        cost_estimate=pl.CostEstimate(flops=flops, bytes_accessed=2**20, transcendentals=0),
    )(*inputs)


def exchange(array, axes):
    return lax.all_to_all(array, axes, split_axis=0, concat_axis=0, tiled=True)


def local(state, gates, gate_qubits, swap_order):
    scalars, vectors, remote = [pltpu.SMEM] * 2, pltpu.VMEM, pl.ANY
    place, done = pltpu.SMEM((16,), I32), pltpu.SemaphoreType.DMA((2,))
    rows = state.reshape(2, ROWS, DIM).transpose(1, 0, 2).reshape(2 * ROWS, DIM)
    sent = call(
        first_kernel,
        (gate_qubits, swap_order, rows, gates),
        jax.ShapeDtypeStruct((2 * ROWS, DIM), F32),
        [*scalars, remote, remote],
        [
            pltpu.VMEM((2 * ROWS, DIM), F32),
            pltpu.VMEM((3, 2, DIM, DIM), F32),
            place,
            done,
        ],
        3 * 10**9,
        LARGE_LIMIT,
    )
    count = lax.axis_size(SENT)
    arrived = exchange(sent.reshape(count, -1, DIM), SENT).reshape(2 * ROWS, DIM)
    matrices = call(
        compose_kernel,
        (gate_qubits, swap_order, gates),
        jax.ShapeDtypeStruct((8 * ROWS, ROWS), BF16),
        [*scalars, vectors],
        [place],
        10**10,
    )
    narrow, others = lax.axis_size("narrow"), lax.axis_size(OTHERS)
    blocks = call(
        middle_kernel,
        (arrived, matrices),
        jax.ShapeDtypeStruct((narrow, 2 * DIM + TAIL, DIM), F32),
        [vectors, pltpu.HBM],
        [pltpu.VMEM((4 * ROWS, ROWS), BF16)] * 2 + [done],
        2 * 10**9,
        MIDDLE_LIMIT,
    )
    returned = exchange(blocks, "narrow")
    extremes = call(
        reduce_kernel,
        (returned,),
        jax.ShapeDtypeStruct((others, DIM), F32),
        [vectors],
    )
    extremes = exchange(extremes.reshape(others, 1, DIM), OTHERS).reshape(others, DIM)
    out = call(
        last_kernel,
        (extremes, returned),
        jax.ShapeDtypeStruct((2 * ROWS, DIM), F32),
        [vectors] * 2,
        (),
        10**7,
    )
    return out.reshape(ROWS, 2, DIM).transpose(1, 0, 2).reshape(2, -1)


def solution(mesh):
    split = Mesh(mesh.devices.reshape(16, 4, 2, mesh.shape["narrow"]), ALL)
    return jax.shard_map(
        local,
        mesh=split,
        in_specs=(P(None, ALL), P(), P(), P()),
        out_specs=P(None, ALL),
        check_vma=False,
    )
```

```python
import functools
import math

import jax
import jax.numpy as jnp
from jax import lax
from jax.experimental import pallas as pl
from jax.experimental.pallas import tpu as pltpu
from jax.sharding import Mesh
from jax.sharding import PartitionSpec as P

LANE_QUBITS = 7
UPPER = 9
ROWS = 2**UPPER
DIM = 128
PART = 32
TAIL = 8
LAST, OTHERS = ("x", "narrow"), ("core", "z")
ALL = ("z", "x", "core", "narrow")
SENT = ("x", "core", "narrow", "z")

F32, BF16, I32 = jnp.float32, jnp.bfloat16, jnp.int32
companding = 16.0
companding_norm = math.log(16.0 + math.sqrt(257.0))
VMEM_LIMIT = 40 * 2**20
MIDDLE_LIMIT = 52 * 2**20
LARGE_LIMIT = 60 * 2**20


def dot(a, b):
    return jnp.dot(a, b, preferred_element_type=F32)


def pieces(x):
    high = x.astype(BF16)
    return high, (x - high.astype(F32)).astype(BF16)


def gate_layout(gate_qubits, gate):
    chosen = [gate_qubits[gate, k] - LANE_QUBITS for k in range(7)]
    used = sum(lax.shift_left(I32(1), c) for c in chosen)
    low, high = I32(0), I32(0)
    for row_bit in range(UPPER):
        free = (lax.shift_right_logical(used, I32(row_bit)) & 1) == 0
        low = jnp.where(free & (high == 0) & (low == 0), row_bit + 100, low)
        high = jnp.where(free, row_bit, high)
    return chosen + [low - 100, high]


def swap_layout(swap_order):
    order = [swap_order[k] - LANE_QUBITS for k in range(UPPER)]
    return order[5:] + order[2:5] + order[:2]


def permutation(source, target, place):
    if target is not None:
        for b in range(UPPER):
            place[target[b]] = I32(b)
    index = lax.broadcasted_iota(I32, (1, ROWS), 1)
    moved = jnp.zeros((1, ROWS), I32)
    for b in range(UPPER):
        row_bit = b if source is None else source[b]
        to = row_bit if target is None else place[row_bit]
        moved = moved + (lax.shift_right_logical(index, b) & 1) * lax.shift_left(I32(1), I32(to))
    rows = lax.broadcasted_iota(I32, (ROWS, ROWS), 0)
    return jnp.where(rows == moved, 1.0, 0.0).astype(BF16)


def gate_matrix(gates_ref, gate):
    real, imag = gates_ref[gate, 0], gates_ref[gate, 1]
    top = jnp.concatenate([real, -imag], axis=1)
    bottom = jnp.concatenate([imag, real], axis=1)
    return pieces(jnp.concatenate([top, bottom], axis=0))


def apply_gate(matrix, high, low):
    width = high.shape[1] // 2

    def stack(part):
        blocks = slabs_of(part)
        real = jnp.concatenate([block[:, :width] for block in blocks], axis=1)
        imag = jnp.concatenate([block[:, width:] for block in blocks], axis=1)
        return jnp.concatenate([real, imag], axis=0)

    upper, lower = matrix
    if low is None:
        left = jnp.concatenate([upper, lower], axis=1)
        right = jnp.concatenate([stack(high)] * 2, axis=0)
    else:
        stacked = stack(high)
        left = jnp.concatenate([upper, upper, lower], axis=1)
        right = jnp.concatenate([stacked, stack(low), stacked], axis=0)
    mixed = dot(left, right)
    columns = [mixed[:, width * i : width * (i + 1)] for i in range(4)]
    return jnp.concatenate(
        [jnp.concatenate([c[:DIM], c[DIM:]], axis=1) for c in columns], axis=0
    )


def permute(matrix, high, low):
    return dot(matrix, high).astype(BF16), dot(matrix, low).astype(BF16)


def slabs_of(x, count=4):
    size = x.shape[0] // count
    return [x[size * i : size * (i + 1)] for i in range(count)]


def exchange_bit(slabs, bit, width):
    lane = lax.broadcasted_iota(I32, slabs[0].shape, 1)
    clear = (lane & width) == 0
    out = list(slabs)
    for i in range(len(slabs)):
        j = i | bit
        if i != j:
            out[i] = jnp.where(clear, slabs[i], pltpu.roll(slabs[j], width, 1))
            out[j] = jnp.where(clear, pltpu.roll(slabs[i], DIM - width, 1), slabs[j])
    return out


def quarters(slabs):
    return exchange_bit(exchange_bit(slabs, 1, 32), 2, 64)


def sixteenths(x):
    slabs = slabs_of(x, 16)
    for k in range(4):
        slabs = exchange_bit(slabs, 1 << k, 8 << k)
    return slabs


def first_kernel(
    gate_qubits, swap_order, state_hbm, gates_hbm, out_ref, state_ref, gates_ref, place, done
):
    state_copy = pltpu.make_async_copy(state_hbm, state_ref, done.at[0])
    gates_copy = pltpu.make_async_copy(gates_hbm.at[pl.ds(0, 3)], gates_ref, done.at[1])
    state_copy.start()
    gates_copy.start()
    targets = [gate_layout(gate_qubits, gate) for gate in range(3)]
    matrix = permutation(None, targets[0], place)
    state_copy.wait()
    planes = [state_ref[pl.ds(p, ROWS, stride=2), :] for p in range(2)]
    high, low = pieces(jnp.concatenate(planes, axis=1))
    high, low = permute(matrix, high, low)
    gates_copy.wait()
    for gate in range(3):
        high, low = pieces(apply_gate(gate_matrix(gates_ref, gate), high, low))
        target = targets[gate + 1] if gate < 2 else swap_layout(swap_order)
        matrix = permutation(targets[gate], target, place)
        if gate < 2:
            high, low = permute(matrix, high, low)
    mixed = dot(matrix, high) + dot(matrix, low)
    for p in range(2):
        for number, slab in enumerate(sixteenths(mixed[:, DIM * p : DIM * (p + 1)])):
            x, y = number // 4, number % 4
            for core in range(2):
                start = 128 * (2 * x + core) + 32 * y + p
                out_ref[pl.ds(start, 16, stride=2), :] = slab[16 * core : 16 * (core + 1)]


def compose_kernel(gate_qubits, swap_order, gates_ref, out_ref, place):
    swapped = swap_layout(swap_order)
    for start, numbers, last in ((0, (3, 4, 5), swapped), (4 * ROWS, (6, 7), None)):
        layout = swapped
        for gate in numbers:
            target = gate_layout(gate_qubits, gate)
            matrix = permutation(layout, target, place)
            if gate == numbers[0]:
                high = jnp.concatenate([matrix, jnp.zeros_like(matrix)], axis=1)
                low = None
            else:
                high, low = permute(matrix, high, low)
            layout = target
            high, low = pieces(apply_gate(gate_matrix(gates_ref, gate), high, low))
        high, low = permute(permutation(layout, last, place), high, low)
        for number, part in enumerate((high[:, :ROWS], high[:, ROWS:], low[:, :ROWS], low[:, ROWS:])):
            out_ref[start + ROWS * number : start + ROWS * (number + 1), :] = part


def apply_matrix(matrix_ref, copies, real, imag):
    high, low = pieces(jnp.concatenate([real, imag], axis=1))
    total = []
    right = jnp.concatenate([high, low], axis=0)
    for number in range(2):
        copies[number].wait()
        part = matrix_ref[ROWS * number : ROWS * (number + 1), :]
        total.append(dot(jnp.concatenate([part, part], axis=1), right))
    for number in range(2):
        copies[number + 2].wait()
        total[number] = total[number] + dot(
            matrix_ref[ROWS * (number + 2) : ROWS * (number + 3), :], high
        )
    return (
        total[0][:, :DIM] - total[1][:, DIM:],
        total[1][:, :DIM] + total[0][:, DIM:],
    )


def middle_kernel(
    arrived_ref, matrices_hbm, out_ref, second_ref, third_ref, done
):
    copies = []
    for number in range(8):
        target = (second_ref, third_ref)[number // 4]
        copies.append(
            pltpu.make_async_copy(
                matrices_hbm.at[pl.ds(ROWS * number, ROWS)],
                target.at[pl.ds(ROWS * (number % 4), ROWS)],
                done.at[number],
            )
        )
        copies[number].start()
    planes = []
    for p in range(2):
        slabs = []
        for n in range(4):
            starts = [128 * block + 32 * n + p for block in range(8)]
            rows = [arrived_ref[pl.ds(start, 16, stride=2), :] for start in starts]
            slabs.append(jnp.concatenate(rows, axis=0))
        planes.append(jnp.concatenate(quarters(slabs), axis=0))
    planes = apply_matrix(second_ref, copies[:4], *planes)
    planes = [jnp.concatenate(quarters(slabs_of(x)), axis=0) for x in planes]
    planes = apply_matrix(third_ref, copies[4:], *planes)
    highest = jnp.max(jnp.maximum(planes[0], planes[1]))
    lowest = jnp.min(jnp.minimum(planes[0], planes[1]))
    lane = lax.broadcasted_iota(I32, (TAIL, DIM), 1)
    extremes = jnp.where(lane < 64, highest, -lowest)
    for p in range(2):
        for number, slab in enumerate(sixteenths(planes[p])):
            target = 4 * (number % 4) + number // 4
            out_ref[target, PART * p : PART * (p + 1), :] = slab
    for target in range(16):
        out_ref[target, 2 * PART : 2 * PART + TAIL, :] = extremes


def reduce_kernel(arrived_ref, out_ref):
    found = jnp.max(
        jnp.max(arrived_ref[:, 2 * PART : 2 * PART + TAIL, :], axis=0), axis=0, keepdims=True
    )
    out_ref[...] = jnp.broadcast_to(found, out_ref.shape)


def last_kernel(extremes_ref, arrived_ref, out_ref):
    lane = lax.broadcasted_iota(I32, extremes_ref.shape, 1)
    found = extremes_ref[...]
    least = jnp.min(found)
    highest = jnp.max(jnp.where(lane < 64, found, least))
    lowest = -jnp.max(jnp.where(lane < 64, least, found))
    middle = (highest + lowest) * 0.5
    halfwidth = (highest - lowest) * 0.5 + 1e-06
    for p in range(2):
        rows = [arrived_ref[n, PART * p : PART * (p + 1), :] for n in range(16)]
        for q, slab in enumerate(sixteenths(jnp.concatenate(rows, axis=0))):
            value = companding * (slab - middle) / halfwidth
            size = jnp.abs(value)
            curve = jnp.log(size + jnp.sqrt(size * size + 1.0)) / companding_norm
            out_ref[pl.ds(2 * PART * q + p, PART, stride=2), :] = jnp.where(value < 0, -curve, curve)


def call(kernel, inputs, outs, places, scratch=(), flops=0, limit=VMEM_LIMIT):
    return pl.pallas_call(
        kernel,
        out_shape=outs,
        in_specs=[pl.BlockSpec(memory_space=m) for m in places],
        scratch_shapes=scratch,
        compiler_params=pltpu.CompilerParams(vmem_limit_bytes=limit),
        cost_estimate=pl.CostEstimate(flops=flops, bytes_accessed=2**20, transcendentals=0),
    )(*inputs)


def exchange(array, axes):
    return lax.all_to_all(array, axes, split_axis=0, concat_axis=0, tiled=True)


def local(state, gates, gate_qubits, swap_order):
    scalars, vectors, remote = [pltpu.SMEM] * 2, pltpu.VMEM, pl.ANY
    place, done = pltpu.SMEM((16,), I32), pltpu.SemaphoreType.DMA((2,))
    rows = state.reshape(2, ROWS, DIM).transpose(1, 0, 2).reshape(2 * ROWS, DIM)
    sent = call(
        first_kernel,
        (gate_qubits, swap_order, rows, gates),
        jax.ShapeDtypeStruct((2 * ROWS, DIM), F32),
        [*scalars, remote, remote],
        [
            pltpu.VMEM((2 * ROWS, DIM), F32),
            pltpu.VMEM((3, 2, DIM, DIM), F32),
            place,
            done,
        ],
        3 * 10**9,
        LARGE_LIMIT,
    )
    count = lax.axis_size(SENT)
    arrived = exchange(sent.reshape(count, -1, DIM), SENT).reshape(2 * ROWS, DIM)
    matrices = call(
        compose_kernel,
        (gate_qubits, swap_order, gates),
        jax.ShapeDtypeStruct((8 * ROWS, ROWS), BF16),
        [*scalars, vectors],
        [place],
        10**10,
    )
    targets, others = lax.axis_size(LAST), lax.axis_size(OTHERS)
    blocks = call(
        middle_kernel,
        (arrived, matrices),
        jax.ShapeDtypeStruct((targets, 2 * PART + TAIL, DIM), F32),
        [vectors, pltpu.HBM],
        [pltpu.VMEM((4 * ROWS, ROWS), BF16)] * 2 + [pltpu.SemaphoreType.DMA((8,))],
        2 * 10**9,
        MIDDLE_LIMIT,
    )
    returned = exchange(blocks, LAST)
    extremes = call(
        reduce_kernel,
        (returned,),
        jax.ShapeDtypeStruct((others, DIM), F32),
        [vectors],
    )
    extremes = exchange(extremes.reshape(others, 1, DIM), OTHERS).reshape(others, DIM)
    out = call(
        last_kernel,
        (extremes, returned),
        jax.ShapeDtypeStruct((2 * ROWS, DIM), F32),
        [vectors] * 2,
        (),
        10**7,
    )
    return out.reshape(ROWS, 2, DIM).transpose(1, 0, 2).reshape(2, -1)


def solution(mesh):
    split = Mesh(mesh.devices.reshape(16, 4, 2, mesh.shape["narrow"]), ALL)
    return jax.shard_map(
        local,
        mesh=split,
        in_specs=(P(None, ALL), P(), P(), P()),
        out_specs=P(None, ALL),
        check_vma=False,
    )
```

```python
import functools
import math

import jax
import jax.numpy as jnp
from jax import lax
from jax.experimental import pallas as pl
from jax.experimental.pallas import tpu as pltpu
from jax.sharding import Mesh
from jax.sharding import PartitionSpec as P

LANE_QUBITS = 7
UPPER = 9
ROWS = 2**UPPER
DIM = 128
PART = 32
TAIL = 8
LAST, OTHERS = ("x", "narrow"), ("core", "z")
ALL = ("z", "x", "core", "narrow")
SENT = ("x", "core", "narrow", "z")
STRIDES = {"x": 128, "core": 64, "narrow": 16, "z": 1}

F32, BF16, I32 = jnp.float32, jnp.bfloat16, jnp.int32
companding = 16.0
companding_norm = math.log(16.0 + math.sqrt(257.0))
VMEM_LIMIT = 40 * 2**20
MIDDLE_LIMIT = 52 * 2**20
LARGE_LIMIT = 60 * 2**20


def dot(a, b):
    return jnp.dot(a, b, preferred_element_type=F32)


def pieces(x):
    high = x.astype(BF16)
    return high, (x - high.astype(F32)).astype(BF16)


def gate_layout(gate_qubits, gate):
    chosen = [gate_qubits[gate, k] - LANE_QUBITS for k in range(7)]
    used = sum(lax.shift_left(I32(1), c) for c in chosen)
    low, high = I32(0), I32(0)
    for row_bit in range(UPPER):
        free = (lax.shift_right_logical(used, I32(row_bit)) & 1) == 0
        low = jnp.where(free & (high == 0) & (low == 0), row_bit + 100, low)
        high = jnp.where(free, row_bit, high)
    return chosen + [low - 100, high]


def swap_layout(swap_order):
    order = [swap_order[k] - LANE_QUBITS for k in range(UPPER)]
    return order[5:] + order[2:5] + order[:2]


def permutation(source, target, place):
    if target is not None:
        for b in range(UPPER):
            place[target[b]] = I32(b)
    index = lax.broadcasted_iota(I32, (1, ROWS), 1)
    moved = jnp.zeros((1, ROWS), I32)
    for b in range(UPPER):
        row_bit = b if source is None else source[b]
        to = row_bit if target is None else place[row_bit]
        moved = moved + (lax.shift_right_logical(index, b) & 1) * lax.shift_left(I32(1), I32(to))
    rows = lax.broadcasted_iota(I32, (ROWS, ROWS), 0)
    return jnp.where(rows == moved, 1.0, 0.0).astype(BF16)


def gate_matrix(gates_ref, gate):
    real, imag = gates_ref[gate, 0], gates_ref[gate, 1]
    top = jnp.concatenate([real, -imag], axis=1)
    bottom = jnp.concatenate([imag, real], axis=1)
    return pieces(jnp.concatenate([top, bottom], axis=0))


def apply_gate(matrix, high, low):
    width = high.shape[1] // 2

    def stack(part):
        blocks = slabs_of(part)
        real = jnp.concatenate([block[:, :width] for block in blocks], axis=1)
        imag = jnp.concatenate([block[:, width:] for block in blocks], axis=1)
        return jnp.concatenate([real, imag], axis=0)

    upper, lower = matrix
    if low is None:
        left = jnp.concatenate([upper, lower], axis=1)
        right = jnp.concatenate([stack(high)] * 2, axis=0)
    else:
        stacked = stack(high)
        left = jnp.concatenate([upper, upper, lower], axis=1)
        right = jnp.concatenate([stacked, stack(low), stacked], axis=0)
    mixed = dot(left, right)
    columns = [mixed[:, width * i : width * (i + 1)] for i in range(4)]
    return jnp.concatenate(
        [jnp.concatenate([c[:DIM], c[DIM:]], axis=1) for c in columns], axis=0
    )


def permute(matrix, high, low):
    return dot(matrix, high).astype(BF16), dot(matrix, low).astype(BF16)


def slabs_of(x, count=4):
    size = x.shape[0] // count
    return [x[size * i : size * (i + 1)] for i in range(count)]


def exchange_bit(slabs, bit, width):
    lane = lax.broadcasted_iota(I32, slabs[0].shape, 1)
    clear = (lane & width) == 0
    out = list(slabs)
    for i in range(len(slabs)):
        j = i | bit
        if i != j:
            out[i] = jnp.where(clear, slabs[i], pltpu.roll(slabs[j], width, 1))
            out[j] = jnp.where(clear, pltpu.roll(slabs[i], DIM - width, 1), slabs[j])
    return out


def quarters(slabs):
    return exchange_bit(exchange_bit(slabs, 1, 32), 2, 64)


def sixteenths(x):
    slabs = slabs_of(x, 16)
    for k in range(4):
        slabs = exchange_bit(slabs, 1 << k, 8 << k)
    return slabs


def block_rows(x, core, narrow, plane):
    start = sum(STRIDES[a] * i for a, i in (("x", x), ("core", core), ("narrow", narrow)))
    return pl.ds(2 * start + plane, 16, stride=2 * STRIDES["z"])


def first_kernel(
    qubits_hbm,
    order_hbm,
    state_hbm,
    gates_hbm,
    out_ref,
    gate_qubits,
    swap_order,
    state_ref,
    gates_ref,
    place,
    done,
):
    qubits_copy = pltpu.make_async_copy(qubits_hbm, gate_qubits, done.at[2])
    order_copy = pltpu.make_async_copy(order_hbm, swap_order, done.at[3])
    qubits_copy.start()
    order_copy.start()
    state_copy = pltpu.make_async_copy(state_hbm, state_ref, done.at[0])
    gates_copy = pltpu.make_async_copy(gates_hbm.at[pl.ds(0, 3)], gates_ref, done.at[1])
    state_copy.start()
    gates_copy.start()
    qubits_copy.wait()
    order_copy.wait()
    targets = [gate_layout(gate_qubits, gate) for gate in range(3)]
    targets.append(swap_layout(swap_order))
    matrix = permutation(None, targets[0], place)
    state_copy.wait()
    planes = [state_ref[pl.ds(p, ROWS, stride=2), :] for p in range(2)]
    high, low = pieces(jnp.concatenate(planes, axis=1))
    high, low = permute(matrix, high, low)
    gates_copy.wait()
    for gate in range(3):
        high, low = pieces(apply_gate(gate_matrix(gates_ref, gate), high, low))
        matrix = permutation(targets[gate], targets[gate + 1], place)
        if gate < 2:
            high, low = permute(matrix, high, low)
    mixed = dot(matrix, high) + dot(matrix, low)
    for p in range(2):
        for number, slab in enumerate(sixteenths(mixed[:, DIM * p : DIM * (p + 1)])):
            x, y = number // 4, number % 4
            for core in range(2):
                rows = slab[16 * core : 16 * (core + 1)]
                out_ref[block_rows(x, core, y, p), :] = rows


def compose_kernel(gate_qubits, swap_order, gates_ref, out_ref, place):
    swapped = swap_layout(swap_order)
    for start, numbers, last in ((0, (3, 4, 5), swapped), (4 * ROWS, (6, 7), None)):
        layout = swapped
        for gate in numbers:
            target = gate_layout(gate_qubits, gate)
            matrix = permutation(layout, target, place)
            if gate == numbers[0]:
                high = jnp.concatenate([matrix, jnp.zeros_like(matrix)], axis=1)
                low = None
            else:
                high, low = permute(matrix, high, low)
            layout = target
            high, low = pieces(apply_gate(gate_matrix(gates_ref, gate), high, low))
        high, low = permute(permutation(layout, last, place), high, low)
        for number, part in enumerate((high[:, :ROWS], high[:, ROWS:], low[:, :ROWS], low[:, ROWS:])):
            out_ref[start + ROWS * number : start + ROWS * (number + 1), :] = part


def apply_matrix(matrix_ref, real, imag):
    high, low = pieces(jnp.concatenate([real, imag], axis=1))
    right = jnp.concatenate([high, low], axis=0)
    total = []
    for number in range(2):
        upper = matrix_ref[ROWS * number : ROWS * (number + 1), :]
        lower = matrix_ref[ROWS * (number + 2) : ROWS * (number + 3), :]
        total.append(dot(jnp.concatenate([upper, upper], axis=1), right) + dot(lower, high))
    return (
        total[0][:, :DIM] - total[1][:, DIM:],
        total[1][:, :DIM] + total[0][:, DIM:],
    )


def middle_kernel(
    arrived_ref, matrices_hbm, out_ref, second_ref, third_ref, done
):
    copies = [
        pltpu.make_async_copy(
            matrices_hbm.at[pl.ds(4 * ROWS * number, 4 * ROWS)], target, done.at[number]
        )
        for number, target in enumerate((second_ref, third_ref))
    ]
    for copy in copies:
        copy.start()
    planes = []
    for p in range(2):
        slabs = []
        for n in range(4):
            rows = [
                arrived_ref[block_rows(block // 2, block % 2, n, p), :] for block in range(8)
            ]
            slabs.append(jnp.concatenate(rows, axis=0))
        planes.append(jnp.concatenate(quarters(slabs), axis=0))
    copies[0].wait()
    planes = apply_matrix(second_ref, *planes)
    planes = [jnp.concatenate(quarters(slabs_of(x)), axis=0) for x in planes]
    copies[1].wait()
    planes = apply_matrix(third_ref, *planes)
    highest = jnp.max(jnp.maximum(planes[0], planes[1]))
    lowest = jnp.min(jnp.minimum(planes[0], planes[1]))
    lane = lax.broadcasted_iota(I32, (TAIL, DIM), 1)
    extremes = jnp.where(lane < 64, highest, -lowest)
    for p in range(2):
        for number, slab in enumerate(sixteenths(planes[p])):
            target = 4 * (number % 4) + number // 4
            out_ref[target, PART * p : PART * (p + 1), :] = slab
    for target in range(16):
        out_ref[target, 2 * PART : 2 * PART + TAIL, :] = extremes


def reduce_kernel(arrived_ref, out_ref):
    found = jnp.max(
        jnp.max(arrived_ref[:, 2 * PART : 2 * PART + TAIL, :], axis=0), axis=0, keepdims=True
    )
    out_ref[...] = jnp.broadcast_to(found, out_ref.shape)


def last_kernel(extremes_ref, arrived_ref, out_ref):
    lane = lax.broadcasted_iota(I32, extremes_ref.shape, 1)
    found = extremes_ref[...]
    least = jnp.min(found)
    highest = jnp.max(jnp.where(lane < 64, found, least))
    lowest = -jnp.max(jnp.where(lane < 64, least, found))
    middle = (highest + lowest) * 0.5
    halfwidth = (highest - lowest) * 0.5 + 1e-06
    scale = jnp.full((8, DIM), companding, F32) / halfwidth
    scale = jnp.concatenate([scale] * (PART // 8), axis=0)
    for p in range(2):
        rows = [arrived_ref[n, PART * p : PART * (p + 1), :] for n in range(16)]
        for q, slab in enumerate(sixteenths(jnp.concatenate(rows, axis=0))):
            value = (slab - middle) * scale
            size = jnp.abs(value)
            curve = jnp.log(size + jnp.sqrt(size * size + 1.0)) * (1.0 / companding_norm)
            out_ref[pl.ds(2 * PART * q + p, PART, stride=2), :] = jnp.where(value < 0, -curve, curve)


def call(kernel, inputs, outs, places, scratch=(), flops=0, limit=VMEM_LIMIT):
    return pl.pallas_call(
        kernel,
        out_shape=outs,
        in_specs=[pl.BlockSpec(memory_space=m) for m in places],
        scratch_shapes=scratch,
        compiler_params=pltpu.CompilerParams(vmem_limit_bytes=limit),
        cost_estimate=pl.CostEstimate(flops=flops, bytes_accessed=2**20, transcendentals=0),
    )(*inputs)


def exchange(array, axes):
    return lax.all_to_all(array, axes, split_axis=0, concat_axis=0, tiled=True)


def local(state, gates, gate_qubits, swap_order):
    scalars, vectors, remote = [pltpu.SMEM] * 2, pltpu.VMEM, pl.ANY
    place, done = pltpu.SMEM((16,), I32), pltpu.SemaphoreType.DMA((4,))
    rows = state.reshape(2, ROWS, DIM).transpose(1, 0, 2).reshape(2 * ROWS, DIM)
    sent = call(
        first_kernel,
        (gate_qubits, swap_order, rows, gates),
        jax.ShapeDtypeStruct((2 * ROWS, DIM), F32),
        [remote] * 4,
        [
            pltpu.SMEM(gate_qubits.shape, I32),
            pltpu.SMEM(swap_order.shape, I32),
            pltpu.VMEM((2 * ROWS, DIM), F32),
            pltpu.VMEM((3, 2, DIM, DIM), F32),
            place,
            done,
        ],
        3 * 10**9,
        LARGE_LIMIT,
    )
    count = lax.axis_size(SENT)
    arrived = exchange(sent.reshape(count, -1, DIM), SENT).reshape(2 * ROWS, DIM)
    matrices = call(
        compose_kernel,
        (gate_qubits, swap_order, gates),
        jax.ShapeDtypeStruct((8 * ROWS, ROWS), BF16),
        [*scalars, vectors],
        [place],
        10**10,
    )
    targets, others = lax.axis_size(LAST), lax.axis_size(OTHERS)
    blocks = call(
        middle_kernel,
        (arrived, matrices),
        jax.ShapeDtypeStruct((targets, 2 * PART + TAIL, DIM), F32),
        [vectors, pltpu.HBM],
        [pltpu.VMEM((4 * ROWS, ROWS), BF16)] * 2 + [pltpu.SemaphoreType.DMA((2,))],
        2 * 10**9,
        MIDDLE_LIMIT,
    )
    returned = exchange(blocks, LAST)
    extremes = call(
        reduce_kernel,
        (returned,),
        jax.ShapeDtypeStruct((others, DIM), F32),
        [vectors],
    )
    extremes = exchange(extremes.reshape(others, 1, DIM), OTHERS).reshape(others, DIM)
    out = call(
        last_kernel,
        (extremes, returned),
        jax.ShapeDtypeStruct((2 * ROWS, DIM), F32),
        [vectors] * 2,
        (),
        10**7,
    )
    return out.reshape(ROWS, 2, DIM).transpose(1, 0, 2).reshape(2, -1)


def solution(mesh):
    split = Mesh(mesh.devices.reshape(16, 4, 2, mesh.shape["narrow"]), ALL)
    return jax.shard_map(
        local,
        mesh=split,
        in_specs=(P(None, ALL), P(), P(), P()),
        out_specs=P(None, ALL),
        check_vma=False,
    )
```

```python
import functools
import math

import jax
import jax.numpy as jnp
from jax import lax
from jax.experimental import pallas as pl
from jax.experimental.pallas import tpu as pltpu
from jax.sharding import Mesh
from jax.sharding import PartitionSpec as P

LANE_QUBITS = 7
UPPER = 9
ROWS = 2**UPPER
DIM = 128
PART = 32
TAIL = 8
LAST, OTHERS = ("x", "narrow"), ("core", "z")
ALL = ("z", "x", "core", "narrow")
SENT = ("x", "core", "narrow", "z")
STRIDES = {"x": 128, "core": 64, "narrow": 16, "z": 1}

F32, BF16, I32 = jnp.float32, jnp.bfloat16, jnp.int32
companding = 16.0
companding_norm = math.log(16.0 + math.sqrt(257.0))
VMEM_LIMIT = 40 * 2**20
MIDDLE_LIMIT = 52 * 2**20
LARGE_LIMIT = 60 * 2**20


def dot(a, b):
    return jnp.dot(a, b, preferred_element_type=F32)


def pieces(x):
    high = x.astype(BF16)
    return high, (x - high.astype(F32)).astype(BF16)


def gate_layout(gate_qubits, gate):
    chosen = [gate_qubits[gate, k] - LANE_QUBITS for k in range(7)]
    used = sum(lax.shift_left(I32(1), c) for c in chosen)
    low, high = I32(0), I32(0)
    for row_bit in range(UPPER):
        free = (lax.shift_right_logical(used, I32(row_bit)) & 1) == 0
        low = jnp.where(free & (high == 0) & (low == 0), row_bit + 100, low)
        high = jnp.where(free, row_bit, high)
    return chosen + [low - 100, high]


def swap_layout(swap_order):
    order = [swap_order[k] - LANE_QUBITS for k in range(UPPER)]
    return order[5:] + order[2:5] + order[:2]


def permutation(source, target, place):
    if target is not None:
        for b in range(UPPER):
            place[target[b]] = I32(b)
    index = lax.broadcasted_iota(I32, (1, ROWS), 1)
    moved = jnp.zeros((1, ROWS), I32)
    for b in range(UPPER):
        row_bit = b if source is None else source[b]
        to = row_bit if target is None else place[row_bit]
        moved = moved + (lax.shift_right_logical(index, b) & 1) * lax.shift_left(I32(1), I32(to))
    rows = lax.broadcasted_iota(I32, (ROWS, ROWS), 0)
    return jnp.where(rows == moved, 1.0, 0.0).astype(BF16)


def gate_matrix(gates_ref, gate):
    real, imag = gates_ref[gate, 0], gates_ref[gate, 1]
    top = jnp.concatenate([real, -imag], axis=1)
    bottom = jnp.concatenate([imag, real], axis=1)
    return pieces(jnp.concatenate([top, bottom], axis=0))


def apply_gate(matrix, high, low):
    width = high.shape[1] // 2

    def stack(part):
        blocks = slabs_of(part)
        real = jnp.concatenate([block[:, :width] for block in blocks], axis=1)
        imag = jnp.concatenate([block[:, width:] for block in blocks], axis=1)
        return jnp.concatenate([real, imag], axis=0)

    upper, lower = matrix
    if low is None:
        left = jnp.concatenate([upper, lower], axis=1)
        right = jnp.concatenate([stack(high)] * 2, axis=0)
    else:
        stacked = stack(high)
        left = jnp.concatenate([upper, upper, lower], axis=1)
        right = jnp.concatenate([stacked, stack(low), stacked], axis=0)
    mixed = dot(left, right)
    columns = [mixed[:, width * i : width * (i + 1)] for i in range(4)]
    return jnp.concatenate(
        [jnp.concatenate([c[:DIM], c[DIM:]], axis=1) for c in columns], axis=0
    )


def permute(matrix, high, low):
    return dot(matrix, high).astype(BF16), dot(matrix, low).astype(BF16)


def slabs_of(x, count=4):
    size = x.shape[0] // count
    return [x[size * i : size * (i + 1)] for i in range(count)]


def exchanged(slabs):
    count = len(slabs)
    width = DIM // count
    lane = lax.broadcasted_iota(I32, slabs[0].shape, 1)
    turned = [pltpu.roll(x, width * i, 1) if i else x for i, x in enumerate(slabs)]
    step = 1
    while step < count:
        moves = (lane & (width * step)) != 0
        turned = [
            jnp.where(moves, turned[(i + step) % count], turned[i]) for i in range(count)
        ]
        step *= 2
    return [
        pltpu.roll(turned[-i % count], DIM - width * i, 1) if i else turned[0]
        for i in range(count)
    ]


def quarters(slabs):
    return exchanged(slabs)


def sixteenths(x):
    return exchanged(slabs_of(x, 16))


def block_rows(x, core, narrow, plane):
    start = sum(STRIDES[a] * i for a, i in (("x", x), ("core", core), ("narrow", narrow)))
    return pl.ds(2 * start + plane, 16, stride=2 * STRIDES["z"])


def first_kernel(
    qubits_hbm,
    order_hbm,
    state_hbm,
    gates_hbm,
    out_ref,
    gate_qubits,
    swap_order,
    state_ref,
    gates_ref,
    place,
    done,
):
    qubits_copy = pltpu.make_async_copy(qubits_hbm, gate_qubits, done.at[2])
    order_copy = pltpu.make_async_copy(order_hbm, swap_order, done.at[3])
    qubits_copy.start()
    order_copy.start()
    state_copy = pltpu.make_async_copy(state_hbm, state_ref, done.at[0])
    gates_copy = pltpu.make_async_copy(gates_hbm.at[pl.ds(0, 3)], gates_ref, done.at[1])
    state_copy.start()
    gates_copy.start()
    qubits_copy.wait()
    order_copy.wait()
    targets = [gate_layout(gate_qubits, gate) for gate in range(3)]
    targets.append(swap_layout(swap_order))
    matrix = permutation(None, targets[0], place)
    state_copy.wait()
    planes = [state_ref[pl.ds(p, ROWS, stride=2), :] for p in range(2)]
    high, low = pieces(jnp.concatenate(planes, axis=1))
    high, low = permute(matrix, high, low)
    gates_copy.wait()
    for gate in range(3):
        high, low = pieces(apply_gate(gate_matrix(gates_ref, gate), high, low))
        matrix = permutation(targets[gate], targets[gate + 1], place)
        if gate < 2:
            high, low = permute(matrix, high, low)
    mixed = dot(matrix, high) + dot(matrix, low)
    for p in range(2):
        for number, slab in enumerate(sixteenths(mixed[:, DIM * p : DIM * (p + 1)])):
            x, y = number // 4, number % 4
            for core in range(2):
                rows = slab[16 * core : 16 * (core + 1)]
                out_ref[block_rows(x, core, y, p), :] = rows


def compose_kernel(gate_qubits, swap_order, gates_ref, out_ref, place):
    swapped = swap_layout(swap_order)
    for start, numbers, last in ((0, (3, 4, 5), swapped), (4 * ROWS, (6, 7), None)):
        layout = swapped
        for gate in numbers:
            target = gate_layout(gate_qubits, gate)
            matrix = permutation(layout, target, place)
            if gate == numbers[0]:
                high = jnp.concatenate([matrix, jnp.zeros_like(matrix)], axis=1)
                low = None
            else:
                high, low = permute(matrix, high, low)
            layout = target
            high, low = pieces(apply_gate(gate_matrix(gates_ref, gate), high, low))
        high, low = permute(permutation(layout, last, place), high, low)
        for number, part in enumerate((high[:, :ROWS], high[:, ROWS:], low[:, :ROWS], low[:, ROWS:])):
            out_ref[start + ROWS * number : start + ROWS * (number + 1), :] = part


def apply_matrix(matrix_ref, real, imag):
    high, low = pieces(jnp.concatenate([real, imag], axis=1))
    right = jnp.concatenate([high, low], axis=0)
    total = []
    for number in range(2):
        upper = matrix_ref[ROWS * number : ROWS * (number + 1), :]
        lower = matrix_ref[ROWS * (number + 2) : ROWS * (number + 3), :]
        total.append(dot(jnp.concatenate([upper, upper], axis=1), right) + dot(lower, high))
    return (
        total[0][:, :DIM] - total[1][:, DIM:],
        total[1][:, :DIM] + total[0][:, DIM:],
    )


def middle_kernel(
    arrived_ref, matrices_hbm, out_ref, second_ref, third_ref, done
):
    copies = [
        pltpu.make_async_copy(
            matrices_hbm.at[pl.ds(4 * ROWS * number, 4 * ROWS)], target, done.at[number]
        )
        for number, target in enumerate((second_ref, third_ref))
    ]
    for copy in copies:
        copy.start()
    planes = []
    for p in range(2):
        slabs = []
        for n in range(4):
            rows = [
                arrived_ref[block_rows(block // 2, block % 2, n, p), :] for block in range(8)
            ]
            slabs.append(jnp.concatenate(rows, axis=0))
        planes.append(jnp.concatenate(quarters(slabs), axis=0))
    copies[0].wait()
    planes = apply_matrix(second_ref, *planes)
    planes = [jnp.concatenate(quarters(slabs_of(x)), axis=0) for x in planes]
    copies[1].wait()
    planes = apply_matrix(third_ref, *planes)
    highest = jnp.max(jnp.maximum(planes[0], planes[1]))
    lowest = jnp.min(jnp.minimum(planes[0], planes[1]))
    lane = lax.broadcasted_iota(I32, (TAIL, DIM), 1)
    extremes = jnp.where(lane < 64, highest, -lowest)
    for p in range(2):
        for number, slab in enumerate(sixteenths(planes[p])):
            target = 4 * (number % 4) + number // 4
            out_ref[target, PART * p : PART * (p + 1), :] = slab
    for target in range(16):
        out_ref[target, 2 * PART : 2 * PART + TAIL, :] = extremes


def reduce_kernel(arrived_ref, out_ref):
    found = jnp.max(
        jnp.max(arrived_ref[:, 2 * PART : 2 * PART + TAIL, :], axis=0), axis=0, keepdims=True
    )
    out_ref[...] = jnp.broadcast_to(found, out_ref.shape)


def last_kernel(extremes_ref, arrived_ref, out_ref):
    lane = lax.broadcasted_iota(I32, extremes_ref.shape, 1)
    found = extremes_ref[...]
    least = jnp.min(found)
    highest = jnp.max(jnp.where(lane < 64, found, least))
    lowest = -jnp.max(jnp.where(lane < 64, least, found))
    middle = (highest + lowest) * 0.5
    halfwidth = (highest - lowest) * 0.5 + 1e-06
    scale = jnp.full((8, DIM), companding, F32) / halfwidth
    scale = jnp.concatenate([scale] * (PART // 8), axis=0)
    for p in range(2):
        rows = [arrived_ref[n, PART * p : PART * (p + 1), :] for n in range(16)]
        for q, slab in enumerate(sixteenths(jnp.concatenate(rows, axis=0))):
            value = (slab - middle) * scale
            size = jnp.abs(value)
            curve = jnp.log(size + jnp.sqrt(size * size + 1.0)) * (1.0 / companding_norm)
            out_ref[pl.ds(2 * PART * q + p, PART, stride=2), :] = jnp.where(value < 0, -curve, curve)


def call(kernel, inputs, outs, places, scratch=(), flops=0, limit=VMEM_LIMIT):
    return pl.pallas_call(
        kernel,
        out_shape=outs,
        in_specs=[pl.BlockSpec(memory_space=m) for m in places],
        scratch_shapes=scratch,
        compiler_params=pltpu.CompilerParams(vmem_limit_bytes=limit),
        cost_estimate=pl.CostEstimate(flops=flops, bytes_accessed=2**20, transcendentals=0),
    )(*inputs)


def exchange(array, axes):
    return lax.all_to_all(array, axes, split_axis=0, concat_axis=0, tiled=True)


def local(state, gates, gate_qubits, swap_order):
    scalars, vectors, remote = [pltpu.SMEM] * 2, pltpu.VMEM, pl.ANY
    place, done = pltpu.SMEM((16,), I32), pltpu.SemaphoreType.DMA((4,))
    rows = state.reshape(2, ROWS, DIM).transpose(1, 0, 2).reshape(2 * ROWS, DIM)
    sent = call(
        first_kernel,
        (gate_qubits, swap_order, rows, gates),
        jax.ShapeDtypeStruct((2 * ROWS, DIM), F32),
        [remote] * 4,
        [
            pltpu.SMEM(gate_qubits.shape, I32),
            pltpu.SMEM(swap_order.shape, I32),
            pltpu.VMEM((2 * ROWS, DIM), F32),
            pltpu.VMEM((3, 2, DIM, DIM), F32),
            place,
            done,
        ],
        3 * 10**9,
        LARGE_LIMIT,
    )
    count = lax.axis_size(SENT)
    arrived = exchange(sent.reshape(count, -1, DIM), SENT).reshape(2 * ROWS, DIM)
    matrices = call(
        compose_kernel,
        (gate_qubits, swap_order, gates),
        jax.ShapeDtypeStruct((8 * ROWS, ROWS), BF16),
        [*scalars, vectors],
        [place],
        10**10,
    )
    targets, others = lax.axis_size(LAST), lax.axis_size(OTHERS)
    blocks = call(
        middle_kernel,
        (arrived, matrices),
        jax.ShapeDtypeStruct((targets, 2 * PART + TAIL, DIM), F32),
        [vectors, pltpu.HBM],
        [pltpu.VMEM((4 * ROWS, ROWS), BF16)] * 2 + [pltpu.SemaphoreType.DMA((2,))],
        2 * 10**9,
        MIDDLE_LIMIT,
    )
    returned = exchange(blocks, LAST)
    extremes = call(
        reduce_kernel,
        (returned,),
        jax.ShapeDtypeStruct((others, DIM), F32),
        [vectors],
    )
    extremes = exchange(extremes.reshape(others, 1, DIM), OTHERS).reshape(others, DIM)
    out = call(
        last_kernel,
        (extremes, returned),
        jax.ShapeDtypeStruct((2 * ROWS, DIM), F32),
        [vectors] * 2,
        (),
        10**7,
    )
    return out.reshape(ROWS, 2, DIM).transpose(1, 0, 2).reshape(2, -1)


def solution(mesh):
    split = Mesh(mesh.devices.reshape(16, 4, 2, mesh.shape["narrow"]), ALL)
    return jax.shard_map(
        local,
        mesh=split,
        in_specs=(P(None, ALL), P(), P(), P()),
        out_specs=P(None, ALL),
        check_vma=False,
    )
```

```python
import functools
import math

import jax
import jax.numpy as jnp
from jax import lax
from jax.experimental import pallas as pl
from jax.experimental.pallas import tpu as pltpu
from jax.sharding import Mesh
from jax.sharding import PartitionSpec as P

LANE_QUBITS = 7
UPPER = 9
ROWS = 2**UPPER
DIM = 128
PART = 32
TAIL = 8
LAST, OTHERS = ("x", "narrow"), ("core", "z")
ALL = ("z", "x", "core", "narrow")
SENT = ("x", "core", "narrow", "z")
STRIDES = {"x": 128, "core": 64, "narrow": 16, "z": 1}

F32, BF16, I32 = jnp.float32, jnp.bfloat16, jnp.int32
companding = 16.0
companding_norm = math.log(16.0 + math.sqrt(257.0))
VMEM_LIMIT = 40 * 2**20
MIDDLE_LIMIT = 52 * 2**20
LARGE_LIMIT = 60 * 2**20


def dot(a, b):
    return jnp.dot(a, b, preferred_element_type=F32)


def pieces(x):
    high = x.astype(BF16)
    return high, (x - high.astype(F32)).astype(BF16)


def gate_layout(gate_qubits, gate):
    chosen = [gate_qubits[gate, k] - LANE_QUBITS for k in range(7)]
    used = sum(lax.shift_left(I32(1), c) for c in chosen)
    low, high = I32(0), I32(0)
    for row_bit in range(UPPER):
        free = (lax.shift_right_logical(used, I32(row_bit)) & 1) == 0
        low = jnp.where(free & (high == 0) & (low == 0), row_bit + 100, low)
        high = jnp.where(free, row_bit, high)
    return chosen + [low - 100, high]


def swap_layout(swap_order):
    order = [swap_order[k] - LANE_QUBITS for k in range(UPPER)]
    return order[5:] + order[2:5] + order[:2]


def permutation(source, target, place):
    if target is not None:
        for b in range(UPPER):
            place[target[b]] = I32(b)
    index = lax.broadcasted_iota(I32, (1, ROWS), 1)
    moved = jnp.zeros((1, ROWS), I32)
    for b in range(UPPER):
        row_bit = b if source is None else source[b]
        to = row_bit if target is None else place[row_bit]
        moved = moved + (lax.shift_right_logical(index, b) & 1) * lax.shift_left(I32(1), I32(to))
    rows = lax.broadcasted_iota(I32, (ROWS, ROWS), 0)
    return jnp.where(rows == moved, 1.0, 0.0).astype(BF16)


def gate_matrix(gates_ref, gate):
    real, imag = gates_ref[gate, 0], gates_ref[gate, 1]
    top = jnp.concatenate([real, -imag], axis=1)
    bottom = jnp.concatenate([imag, real], axis=1)
    return pieces(jnp.concatenate([top, bottom], axis=0))


def apply_gate(matrix, high, low):
    width = high.shape[1] // 2

    def stack(part):
        blocks = slabs_of(part)
        real = jnp.concatenate([block[:, :width] for block in blocks], axis=1)
        imag = jnp.concatenate([block[:, width:] for block in blocks], axis=1)
        return jnp.concatenate([real, imag], axis=0)

    upper, lower = matrix
    if low is None:
        left = jnp.concatenate([upper, lower], axis=1)
        right = jnp.concatenate([stack(high)] * 2, axis=0)
    else:
        stacked = stack(high)
        left = jnp.concatenate([upper, upper, lower], axis=1)
        right = jnp.concatenate([stacked, stack(low), stacked], axis=0)
    mixed = dot(left, right)
    columns = [mixed[:, width * i : width * (i + 1)] for i in range(4)]
    return jnp.concatenate(
        [jnp.concatenate([c[:DIM], c[DIM:]], axis=1) for c in columns], axis=0
    )


def permute(matrix, high, low):
    blocks = [matrix[:256], matrix[256:]]
    return tuple(
        jnp.concatenate([dot(block, part).astype(BF16) for block in blocks], axis=0)
        for part in (high, low)
    )


def slabs_of(x, count=4):
    size = x.shape[0] // count
    return [x[size * i : size * (i + 1)] for i in range(count)]


def exchanged(slabs):
    count = len(slabs)
    width = DIM // count
    lane = lax.broadcasted_iota(I32, slabs[0].shape, 1)
    turned = [pltpu.roll(x, width * i, 1) if i else x for i, x in enumerate(slabs)]
    step = 1
    while step < count:
        moves = (lane & (width * step)) != 0
        turned = [
            jnp.where(moves, turned[(i + step) % count], turned[i]) for i in range(count)
        ]
        step *= 2
    return [
        pltpu.roll(turned[-i % count], DIM - width * i, 1) if i else turned[0]
        for i in range(count)
    ]


def quarters(slabs):
    return exchanged(slabs)


def sixteenths(x):
    return exchanged(slabs_of(x, 16))


def block_rows(x, core, narrow, plane):
    start = sum(STRIDES[a] * i for a, i in (("x", x), ("core", core), ("narrow", narrow)))
    return pl.ds(2 * start + plane, 16, stride=2 * STRIDES["z"])


def first_kernel(
    qubits_hbm,
    order_hbm,
    state_hbm,
    gates_hbm,
    out_ref,
    gate_qubits,
    swap_order,
    state_ref,
    gates_ref,
    place,
    done,
):
    qubits_copy = pltpu.make_async_copy(qubits_hbm, gate_qubits, done.at[2])
    order_copy = pltpu.make_async_copy(order_hbm, swap_order, done.at[3])
    qubits_copy.start()
    order_copy.start()
    state_copy = pltpu.make_async_copy(state_hbm, state_ref, done.at[0])
    gates_copy = pltpu.make_async_copy(gates_hbm.at[pl.ds(0, 3)], gates_ref, done.at[1])
    state_copy.start()
    gates_copy.start()
    qubits_copy.wait()
    order_copy.wait()
    targets = [gate_layout(gate_qubits, gate) for gate in range(3)]
    targets.append(swap_layout(swap_order))
    matrix = permutation(None, targets[0], place)
    state_copy.wait()
    planes = [state_ref[pl.ds(p, ROWS, stride=2), :] for p in range(2)]
    high, low = pieces(jnp.concatenate(planes, axis=1))
    high, low = permute(matrix, high, low)
    gates_copy.wait()
    for gate in range(3):
        high, low = pieces(apply_gate(gate_matrix(gates_ref, gate), high, low))
        matrix = permutation(targets[gate], targets[gate + 1], place)
        if gate < 2:
            high, low = permute(matrix, high, low)
    mixed = dot(matrix, high) + dot(matrix, low)
    for p in range(2):
        for number, slab in enumerate(sixteenths(mixed[:, DIM * p : DIM * (p + 1)])):
            x, y = number // 4, number % 4
            for core in range(2):
                rows = slab[16 * core : 16 * (core + 1)]
                out_ref[block_rows(x, core, y, p), :] = rows


def compose_kernel(gate_qubits, swap_order, gates_ref, out_ref, place):
    swapped = swap_layout(swap_order)
    for start, numbers, last in ((0, (3, 4, 5), swapped), (4 * ROWS, (6, 7), None)):
        layout = swapped
        for gate in numbers:
            target = gate_layout(gate_qubits, gate)
            matrix = permutation(layout, target, place)
            if gate == numbers[0]:
                high = jnp.concatenate([matrix, jnp.zeros_like(matrix)], axis=1)
                low = None
            else:
                high, low = permute(matrix, high, low)
            layout = target
            high, low = pieces(apply_gate(gate_matrix(gates_ref, gate), high, low))
        high, low = permute(permutation(layout, last, place), high, low)
        for number, part in enumerate((high[:, :ROWS], high[:, ROWS:], low[:, :ROWS], low[:, ROWS:])):
            out_ref[start + ROWS * number : start + ROWS * (number + 1), :] = part


def apply_matrix(matrix_ref, real, imag):
    high, low = pieces(jnp.concatenate([real, imag], axis=1))
    right = jnp.concatenate([high, low], axis=0)
    total = []
    for number in range(2):
        upper = matrix_ref[ROWS * number : ROWS * (number + 1), :]
        lower = matrix_ref[ROWS * (number + 2) : ROWS * (number + 3), :]
        total.append(dot(jnp.concatenate([upper, upper], axis=1), right) + dot(lower, high))
    return (
        total[0][:, :DIM] - total[1][:, DIM:],
        total[1][:, :DIM] + total[0][:, DIM:],
    )


def middle_kernel(
    arrived_ref, matrices_hbm, out_ref, second_ref, third_ref, done
):
    copies = [
        pltpu.make_async_copy(
            matrices_hbm.at[pl.ds(4 * ROWS * number, 4 * ROWS)], target, done.at[number]
        )
        for number, target in enumerate((second_ref, third_ref))
    ]
    for copy in copies:
        copy.start()
    planes = []
    for p in range(2):
        slabs = []
        for n in range(4):
            rows = [
                arrived_ref[block_rows(block // 2, block % 2, n, p), :] for block in range(8)
            ]
            slabs.append(jnp.concatenate(rows, axis=0))
        planes.append(jnp.concatenate(quarters(slabs), axis=0))
    copies[0].wait()
    planes = apply_matrix(second_ref, *planes)
    planes = [jnp.concatenate(quarters(slabs_of(x)), axis=0) for x in planes]
    copies[1].wait()
    planes = apply_matrix(third_ref, *planes)
    highest = jnp.max(jnp.maximum(planes[0], planes[1]))
    lowest = jnp.min(jnp.minimum(planes[0], planes[1]))
    lane = lax.broadcasted_iota(I32, (TAIL, DIM), 1)
    extremes = jnp.where(lane < 64, highest, -lowest)
    for p in range(2):
        for number, slab in enumerate(sixteenths(planes[p])):
            target = 4 * (number % 4) + number // 4
            out_ref[target, PART * p : PART * (p + 1), :] = slab
    for target in range(16):
        out_ref[target, 2 * PART : 2 * PART + TAIL, :] = extremes


def reduce_kernel(arrived_ref, out_ref):
    found = jnp.max(
        jnp.max(arrived_ref[:, 2 * PART : 2 * PART + TAIL, :], axis=0), axis=0, keepdims=True
    )
    out_ref[...] = jnp.broadcast_to(found, out_ref.shape)


def last_kernel(extremes_ref, arrived_ref, out_ref):
    lane = lax.broadcasted_iota(I32, extremes_ref.shape, 1)
    found = extremes_ref[...]
    least = jnp.min(found)
    highest = jnp.max(jnp.where(lane < 64, found, least))
    lowest = -jnp.max(jnp.where(lane < 64, least, found))
    middle = (highest + lowest) * 0.5
    halfwidth = (highest - lowest) * 0.5 + 1e-06
    scale = jnp.full((8, DIM), companding, F32) / halfwidth
    scale = jnp.concatenate([scale] * (PART // 8), axis=0)
    for p in range(2):
        rows = [arrived_ref[n, PART * p : PART * (p + 1), :] for n in range(16)]
        for q, slab in enumerate(sixteenths(jnp.concatenate(rows, axis=0))):
            value = (slab - middle) * scale
            size = jnp.abs(value)
            curve = jnp.log(size + jnp.sqrt(size * size + 1.0)) * (1.0 / companding_norm)
            out_ref[pl.ds(2 * PART * q + p, PART, stride=2), :] = jnp.where(value < 0, -curve, curve)


def call(kernel, inputs, outs, places, scratch=(), flops=0, limit=VMEM_LIMIT):
    return pl.pallas_call(
        kernel,
        out_shape=outs,
        in_specs=[pl.BlockSpec(memory_space=m) for m in places],
        scratch_shapes=scratch,
        compiler_params=pltpu.CompilerParams(vmem_limit_bytes=limit),
        cost_estimate=pl.CostEstimate(flops=flops, bytes_accessed=2**20, transcendentals=0),
    )(*inputs)


def exchange(array, axes):
    return lax.all_to_all(array, axes, split_axis=0, concat_axis=0, tiled=True)


def local(state, gates, gate_qubits, swap_order):
    scalars, vectors, remote = [pltpu.SMEM] * 2, pltpu.VMEM, pl.ANY
    place, done = pltpu.SMEM((16,), I32), pltpu.SemaphoreType.DMA((4,))
    rows = state.reshape(2, ROWS, DIM).transpose(1, 0, 2).reshape(2 * ROWS, DIM)
    sent = call(
        first_kernel,
        (gate_qubits, swap_order, rows, gates),
        jax.ShapeDtypeStruct((2 * ROWS, DIM), F32),
        [remote] * 4,
        [
            pltpu.SMEM(gate_qubits.shape, I32),
            pltpu.SMEM(swap_order.shape, I32),
            pltpu.VMEM((2 * ROWS, DIM), F32),
            pltpu.VMEM((3, 2, DIM, DIM), F32),
            place,
            done,
        ],
        3 * 10**9,
        LARGE_LIMIT,
    )
    count = lax.axis_size(SENT)
    arrived = exchange(sent.reshape(count, -1, DIM), SENT).reshape(2 * ROWS, DIM)
    matrices = call(
        compose_kernel,
        (gate_qubits, swap_order, gates),
        jax.ShapeDtypeStruct((8 * ROWS, ROWS), BF16),
        [*scalars, vectors],
        [place],
        10**10,
    )
    targets, others = lax.axis_size(LAST), lax.axis_size(OTHERS)
    blocks = call(
        middle_kernel,
        (arrived, matrices),
        jax.ShapeDtypeStruct((targets, 2 * PART + TAIL, DIM), F32),
        [vectors, pltpu.HBM],
        [pltpu.VMEM((4 * ROWS, ROWS), BF16)] * 2 + [pltpu.SemaphoreType.DMA((2,))],
        2 * 10**9,
        MIDDLE_LIMIT,
    )
    returned = exchange(blocks, LAST)
    extremes = call(
        reduce_kernel,
        (returned,),
        jax.ShapeDtypeStruct((others, DIM), F32),
        [vectors],
    )
    extremes = exchange(extremes.reshape(others, 1, DIM), OTHERS).reshape(others, DIM)
    out = call(
        last_kernel,
        (extremes, returned),
        jax.ShapeDtypeStruct((2 * ROWS, DIM), F32),
        [vectors] * 2,
        (),
        10**7,
    )
    return out.reshape(ROWS, 2, DIM).transpose(1, 0, 2).reshape(2, -1)


def solution(mesh):
    split = Mesh(mesh.devices.reshape(16, 4, 2, mesh.shape["narrow"]), ALL)
    return jax.shard_map(
        local,
        mesh=split,
        in_specs=(P(None, ALL), P(), P(), P()),
        out_specs=P(None, ALL),
        check_vma=False,
    )
```

```python
import functools
import math

import jax
import jax.numpy as jnp
from jax import lax
from jax.experimental import pallas as pl
from jax.experimental.pallas import tpu as pltpu
from jax.sharding import Mesh
from jax.sharding import PartitionSpec as P

LANE_QUBITS = 7
UPPER = 9
ROWS = 2**UPPER
DIM = 128
PART = 32
TAIL = 8
LAST, OTHERS = ("x", "narrow"), ("core", "z")
ALL = ("z", "x", "core", "narrow")
SENT = ("x", "core", "narrow", "z")
STRIDES = {"x": 128, "core": 64, "narrow": 16, "z": 1}

F32, BF16, I32 = jnp.float32, jnp.bfloat16, jnp.int32
companding = 16.0
companding_norm = math.log(16.0 + math.sqrt(257.0))
VMEM_LIMIT = 40 * 2**20
MIDDLE_LIMIT = 52 * 2**20
LARGE_LIMIT = 60 * 2**20


def dot(a, b):
    return jnp.dot(a, b, preferred_element_type=F32)


def pieces(x):
    high = x.astype(BF16)
    return high, (x - high.astype(F32)).astype(BF16)


def gate_layout(gate_qubits, gate):
    chosen = [gate_qubits[gate, k] - LANE_QUBITS for k in range(7)]
    used = sum(lax.shift_left(I32(1), c) for c in chosen)
    low, high = I32(0), I32(0)
    for row_bit in range(UPPER):
        free = (lax.shift_right_logical(used, I32(row_bit)) & 1) == 0
        low = jnp.where(free & (high == 0) & (low == 0), row_bit + 100, low)
        high = jnp.where(free, row_bit, high)
    return chosen + [low - 100, high]


def swap_layout(swap_order):
    order = [swap_order[k] - LANE_QUBITS for k in range(UPPER)]
    return order[5:] + order[2:5] + order[:2]


def permutation(source, target, place):
    if target is not None:
        for b in range(UPPER):
            place[target[b]] = I32(b)
    index = lax.broadcasted_iota(I32, (1, ROWS), 1)
    moved = jnp.zeros((1, ROWS), I32)
    for b in range(UPPER):
        row_bit = b if source is None else source[b]
        to = row_bit if target is None else place[row_bit]
        moved = moved + (lax.shift_right_logical(index, b) & 1) * lax.shift_left(I32(1), I32(to))
    rows = lax.broadcasted_iota(I32, (ROWS, ROWS), 0)
    return jnp.where(rows == moved, 1.0, 0.0).astype(BF16)


def gate_matrix(gates_ref, gate):
    real, imag = gates_ref[gate, 0], gates_ref[gate, 1]
    top = jnp.concatenate([real, -imag], axis=1)
    bottom = jnp.concatenate([imag, real], axis=1)
    return pieces(jnp.concatenate([top, bottom], axis=0))


def apply_gate(matrix, high, low):
    width = high.shape[1] // 2

    def stack(part):
        blocks = slabs_of(part)
        real = jnp.concatenate([block[:, :width] for block in blocks], axis=1)
        imag = jnp.concatenate([block[:, width:] for block in blocks], axis=1)
        return jnp.concatenate([real, imag], axis=0)

    upper, lower = matrix
    if low is None:
        left = jnp.concatenate([upper, lower], axis=1)
        right = jnp.concatenate([stack(high)] * 2, axis=0)
    else:
        stacked = stack(high)
        left = jnp.concatenate([upper, upper, lower], axis=1)
        right = jnp.concatenate([stacked, stack(low), stacked], axis=0)
    mixed = dot(left, right)
    columns = [mixed[:, width * i : width * (i + 1)] for i in range(4)]
    return jnp.concatenate(
        [jnp.concatenate([c[:DIM], c[DIM:]], axis=1) for c in columns], axis=0
    )


def permute(matrix, high, low):
    blocks = [matrix[:256], matrix[256:]]
    return tuple(
        jnp.concatenate([dot(block, part).astype(BF16) for block in blocks], axis=0)
        for part in (high, low)
    )


def slabs_of(x, count=4):
    size = x.shape[0] // count
    return [x[size * i : size * (i + 1)] for i in range(count)]


def exchanged(slabs):
    count = len(slabs)
    width = DIM // count
    lane = lax.broadcasted_iota(I32, slabs[0].shape, 1)
    turned = [pltpu.roll(x, width * i, 1) if i else x for i, x in enumerate(slabs)]
    step = 1
    while step < count:
        moves = (lane & (width * step)) != 0
        turned = [
            jnp.where(moves, turned[(i + step) % count], turned[i]) for i in range(count)
        ]
        step *= 2
    return [
        pltpu.roll(turned[-i % count], DIM - width * i, 1) if i else turned[0]
        for i in range(count)
    ]


def quarters(slabs):
    return exchanged(slabs)


def sixteenths(x):
    return exchanged(slabs_of(x, 16))


def block_rows(x, core, narrow, plane):
    start = sum(STRIDES[a] * i for a, i in (("x", x), ("core", core), ("narrow", narrow)))
    return pl.ds(2 * start + plane, 16, stride=2 * STRIDES["z"])


def first_kernel(
    qubits_hbm,
    order_hbm,
    state_hbm,
    gates_hbm,
    out_ref,
    gate_qubits,
    swap_order,
    state_ref,
    gates_ref,
    place,
    done,
):
    qubits_copy = pltpu.make_async_copy(qubits_hbm, gate_qubits, done.at[2])
    order_copy = pltpu.make_async_copy(order_hbm, swap_order, done.at[3])
    qubits_copy.start()
    order_copy.start()
    state_copy = pltpu.make_async_copy(state_hbm, state_ref, done.at[0])
    gates_copy = pltpu.make_async_copy(gates_hbm.at[pl.ds(0, 3)], gates_ref, done.at[1])
    state_copy.start()
    gates_copy.start()
    qubits_copy.wait()
    order_copy.wait()
    targets = [gate_layout(gate_qubits, gate) for gate in range(3)]
    targets.append(swap_layout(swap_order))
    matrix = permutation(None, targets[0], place)
    state_copy.wait()
    planes = [state_ref[pl.ds(p, ROWS, stride=2), :] for p in range(2)]
    high, low = pieces(jnp.concatenate(planes, axis=1))
    high, low = permute(matrix, high, low)
    gates_copy.wait()
    for gate in range(3):
        high, low = pieces(apply_gate(gate_matrix(gates_ref, gate), high, low))
        matrix = permutation(targets[gate], targets[gate + 1], place)
        if gate < 2:
            high, low = permute(matrix, high, low)
    mixed = dot(matrix, high) + dot(matrix, low)
    for p in range(2):
        for number, slab in enumerate(sixteenths(mixed[:, DIM * p : DIM * (p + 1)])):
            x, y = number // 4, number % 4
            for core in range(2):
                rows = slab[16 * core : 16 * (core + 1)]
                out_ref[block_rows(x, core, y, p), :] = rows


def compose_kernel(gate_qubits, swap_order, gates_ref, out_ref, place):
    swapped = swap_layout(swap_order)
    for start, numbers, last in ((0, (3, 4, 5), swapped), (4 * ROWS, (6, 7), None)):
        layout = swapped
        for gate in numbers:
            target = gate_layout(gate_qubits, gate)
            matrix = permutation(layout, target, place)
            if gate == numbers[0]:
                high = jnp.concatenate([matrix, jnp.zeros_like(matrix)], axis=1)
                low = None
            else:
                high, low = permute(matrix, high, low)
            layout = target
            high, low = pieces(apply_gate(gate_matrix(gates_ref, gate), high, low))
        high, low = permute(permutation(layout, last, place), high, low)
        for number, part in enumerate((high[:, :ROWS], low[:, :ROWS], high[:, ROWS:], low[:, ROWS:])):
            out_ref[start + ROWS * number : start + ROWS * (number + 1), :] = part


def apply_matrix(matrix_ref, copies, real, imag):
    high, low = pieces(jnp.concatenate([real, imag], axis=1))
    right = jnp.concatenate([high, low, high], axis=0)
    total = []
    for number in range(2):
        if number < len(copies):
            copies[number].wait()
        rows = []
        for start in range(2 * ROWS * number, 2 * ROWS * number + ROWS, 128):
            upper = matrix_ref[start : start + 128, :]
            lower = matrix_ref[start + ROWS : start + ROWS + 128, :]
            rows.append(dot(jnp.concatenate([upper, upper, lower], axis=1), right))
        total.append(jnp.concatenate(rows, axis=0))
    return (
        total[0][:, :DIM] - total[1][:, DIM:],
        total[1][:, :DIM] + total[0][:, DIM:],
    )


def middle_kernel(
    arrived_ref, matrices_hbm, out_ref, second_ref, third_ref, done
):
    copies = [
        pltpu.make_async_copy(
            matrices_hbm.at[pl.ds(start, size)], target, done.at[number]
        )
        for number, (start, size, target) in enumerate(
            (
                (0, 2 * ROWS, second_ref.at[pl.ds(0, 2 * ROWS)]),
                (2 * ROWS, 2 * ROWS, second_ref.at[pl.ds(2 * ROWS, 2 * ROWS)]),
                (4 * ROWS, 4 * ROWS, third_ref),
            )
        )
    ]
    for copy in copies:
        copy.start()
    planes = []
    for p in range(2):
        slabs = []
        for n in range(4):
            rows = [
                arrived_ref[block_rows(block // 2, block % 2, n, p), :] for block in range(8)
            ]
            slabs.append(jnp.concatenate(rows, axis=0))
        planes.append(jnp.concatenate(quarters(slabs), axis=0))
    planes = apply_matrix(second_ref, copies[:2], *planes)
    planes = [jnp.concatenate(quarters(slabs_of(x)), axis=0) for x in planes]
    planes = apply_matrix(third_ref, copies[2:], *planes)
    highest = jnp.max(jnp.maximum(planes[0], planes[1]))
    lowest = jnp.min(jnp.minimum(planes[0], planes[1]))
    lane = lax.broadcasted_iota(I32, (TAIL, DIM), 1)
    extremes = jnp.where(lane < 64, highest, -lowest)
    for p in range(2):
        for number, slab in enumerate(sixteenths(planes[p])):
            target = 4 * (number % 4) + number // 4
            out_ref[target, PART * p : PART * (p + 1), :] = slab
    for target in range(16):
        out_ref[target, 2 * PART : 2 * PART + TAIL, :] = extremes


def reduce_kernel(arrived_ref, out_ref):
    found = jnp.max(
        jnp.max(arrived_ref[:, 2 * PART : 2 * PART + TAIL, :], axis=0), axis=0, keepdims=True
    )
    out_ref[...] = jnp.broadcast_to(found, out_ref.shape)


def last_kernel(extremes_ref, arrived_ref, out_ref):
    lane = lax.broadcasted_iota(I32, extremes_ref.shape, 1)
    found = extremes_ref[...]
    least = jnp.min(found)
    highest = jnp.max(jnp.where(lane < 64, found, least))
    lowest = -jnp.max(jnp.where(lane < 64, least, found))
    middle = (highest + lowest) * 0.5
    halfwidth = (highest - lowest) * 0.5 + 1e-06
    scale = jnp.full((8, DIM), companding, F32) / halfwidth
    scale = jnp.concatenate([scale] * (PART // 8), axis=0)
    for p in range(2):
        rows = [arrived_ref[n, PART * p : PART * (p + 1), :] for n in range(16)]
        for q, slab in enumerate(sixteenths(jnp.concatenate(rows, axis=0))):
            value = (slab - middle) * scale
            size = jnp.abs(value)
            curve = jnp.log(size + jnp.sqrt(size * size + 1.0)) * (1.0 / companding_norm)
            out_ref[pl.ds(2 * PART * q + p, PART, stride=2), :] = jnp.where(value < 0, -curve, curve)


def call(kernel, inputs, outs, places, scratch=(), flops=0, limit=VMEM_LIMIT):
    return pl.pallas_call(
        kernel,
        out_shape=outs,
        in_specs=[pl.BlockSpec(memory_space=m) for m in places],
        scratch_shapes=scratch,
        compiler_params=pltpu.CompilerParams(vmem_limit_bytes=limit),
        cost_estimate=pl.CostEstimate(flops=flops, bytes_accessed=2**20, transcendentals=0),
    )(*inputs)


def exchange(array, axes):
    return lax.all_to_all(array, axes, split_axis=0, concat_axis=0, tiled=True)


def local(state, gates, gate_qubits, swap_order):
    scalars, vectors, remote = [pltpu.SMEM] * 2, pltpu.VMEM, pl.ANY
    place, done = pltpu.SMEM((16,), I32), pltpu.SemaphoreType.DMA((4,))
    rows = state.reshape(2, ROWS, DIM).transpose(1, 0, 2).reshape(2 * ROWS, DIM)
    sent = call(
        first_kernel,
        (gate_qubits, swap_order, rows, gates),
        jax.ShapeDtypeStruct((2 * ROWS, DIM), F32),
        [remote] * 4,
        [
            pltpu.SMEM(gate_qubits.shape, I32),
            pltpu.SMEM(swap_order.shape, I32),
            pltpu.VMEM((2 * ROWS, DIM), F32),
            pltpu.VMEM((3, 2, DIM, DIM), F32),
            place,
            done,
        ],
        3 * 10**9,
        LARGE_LIMIT,
    )
    count = lax.axis_size(SENT)
    arrived = exchange(sent.reshape(count, -1, DIM), SENT).reshape(2 * ROWS, DIM)
    matrices = call(
        compose_kernel,
        (gate_qubits, swap_order, gates),
        jax.ShapeDtypeStruct((8 * ROWS, ROWS), BF16),
        [*scalars, vectors],
        [place],
        10**10,
    )
    targets, others = lax.axis_size(LAST), lax.axis_size(OTHERS)
    blocks = call(
        middle_kernel,
        (arrived, matrices),
        jax.ShapeDtypeStruct((targets, 2 * PART + TAIL, DIM), F32),
        [vectors, pltpu.HBM],
        [pltpu.VMEM((4 * ROWS, ROWS), BF16)] * 2 + [pltpu.SemaphoreType.DMA((3,))],
        2 * 10**9,
        MIDDLE_LIMIT,
    )
    returned = exchange(blocks, LAST)
    extremes = call(
        reduce_kernel,
        (returned,),
        jax.ShapeDtypeStruct((others, DIM), F32),
        [vectors],
    )
    extremes = exchange(extremes.reshape(others, 1, DIM), OTHERS).reshape(others, DIM)
    out = call(
        last_kernel,
        (extremes, returned),
        jax.ShapeDtypeStruct((2 * ROWS, DIM), F32),
        [vectors] * 2,
        (),
        10**7,
    )
    return out.reshape(ROWS, 2, DIM).transpose(1, 0, 2).reshape(2, -1)


def solution(mesh):
    split = Mesh(mesh.devices.reshape(16, 4, 2, mesh.shape["narrow"]), ALL)
    return jax.shard_map(
        local,
        mesh=split,
        in_specs=(P(None, ALL), P(), P(), P()),
        out_specs=P(None, ALL),
        check_vma=False,
    )
```
